32 devices in a mesh: section: 2 (over core), ctx: 4 (over z), wa: 4 (over y, x).
Axes of the slice: x: 2, y: 2, z: 4, core: 2. Of those that a mesh axis runs over, the one named last changes fastest.
Arguments:
- block_input: bfloat16 [2, 2048, 960], P(None, ('ctx', 'wa')), may hold values from -6 to 6
- out_cotangent: bfloat16 [2, 2048, 960], P(None, ('ctx', 'wa')), may hold values from -6 to 6
- block_table: int32 [32], replicated, may hold values from 0 to 31, as said below
- attn_gain: bfloat16 [2, 960], P('section', 'wa'), may hold values from 0.099609375 to 1.8984375
- w_qkv: bfloat16 [2, 960, 1600], P('section', 'wa'), may hold values from -0.1875 to 0.1875
- w_out: bfloat16 [2, 960, 960], P('section', 'wa'), may hold values from -6 to 6
- mlp_gain: bfloat16 [2, 960], P('section', 'wa'), may hold values from 0.099609375 to 1.8984375
- w_gate: bfloat16 [2, 960, 2560], P('section', 'wa'), may hold values from -0.1875 to 0.1875
- w_up: bfloat16 [2, 960, 2560], P('section', 'wa'), may hold values from -0.1875 to 0.1875
- w_down: bfloat16 [2, 2560, 960], P('section', 'wa'), may hold values from -0.125 to 0.125
Outputs:
- layer_outputs: bfloat16 [2, 2, 2048, 960], P('section', None, ('ctx', 'wa'))
- input_grads: bfloat16 [2, 2, 2048, 960], P('section', None, ('ctx', 'wa'))
- attn_gain_grad: float32 [2, 960], P('section', 'wa')
- w_qkv_grad: float32 [2, 960, 1600], P('section', 'wa')
- w_out_grad: float32 [2, 960, 960], P('section', 'wa')
- mlp_gain_grad: float32 [2, 960], P('section', 'wa')
- w_gate_grad: float32 [2, 960, 2560], P('section', 'wa')
- w_up_grad: float32 [2, 960, 2560], P('section', 'wa')
- w_down_grad: float32 [2, 2560, 960], P('section', 'wa')
The draws below stay inside these ranges and needn't reach their ends.
Inputs may be any that keep to these rules, and one draw needn't show every extreme that they name: `block_table`: stored blocks 2j and 2j+1 hold positional blocks b and 31 - b for some b, in either order; every positional block is held once.
All inputs are finite; a program needn't handle non-finite values.
Results may differ from the reference program's by a relative error of at most 0.015.
Values may be sent and summed in bfloat16 or wider, within the bound.
No kernel may reach another device: no remote copies, remote signals or barrier semaphores. Data moves between devices by JAX's collectives and lax.ppermute only.
A program may use at most 256 MiB of HBM per device.

```python
import math
import jax
import jax.numpy as jnp
from jax import lax

D = 960
H = 15
KVH = 5
HD = 64
FF = 2560
MICRO = 2
QDIM = 960
QKV = 1600
BLOCKS = 32
SEQ = 2048
N_SECTION = 2


def draw_block_table(key, part):
    key = jax.random.fold_in(key, 7)
    order_key, side_key = jax.random.split(key)
    device_count = BLOCKS // 2
    paired = jax.random.permutation(order_key, device_count).astype(jnp.int32)
    flipped = jax.random.randint(side_key, (device_count,), 0, 2, dtype=jnp.int32)
    front_block = jnp.where(flipped == 1, BLOCKS - 1 - paired, paired)
    back_block = BLOCKS - 1 - front_block
    return jnp.stack([front_block, back_block], axis=1).reshape(BLOCKS).astype(jnp.int32)


def steps_of(key, shape, cuts, least, high):
    loudness, own = 1.0, jax.random.fold_in(key, 6)
    for dim, blocks in cuts:
        steps = jnp.exp(jax.random.uniform(jax.random.fold_in(own, dim), (blocks,), jnp.float32, least / len(cuts), high / len(cuts)))
        loudness = loudness * jnp.repeat(steps, shape[dim] // blocks).reshape([-1 if axis == dim else 1 for axis in range(len(shape))])
    return loudness


def scatter_about(key, dims, scale, bound, cuts=(), kind=jnp.bfloat16):
    values = scale * jax.random.normal(key, dims, jnp.float32)
    if cuts:
        values = values * steps_of(key, dims, cuts, -0.22, 0.18)
    return jnp.clip(values, -bound, bound).astype(kind)


def setup_inputs(seed: int = 0) -> dict:
    arg_keys = jax.random.split(jax.random.key(seed), 11)
    block_input = scatter_about(arg_keys[0], (MICRO, SEQ, D), 1.0, 6.0, ((1, 16),))
    out_cotangent = scatter_about(arg_keys[1], (MICRO, SEQ, D), 1.0, 6.0, ((1, 16),))
    block_table = draw_block_table(jax.random.fold_in(arg_keys[10], 71), 0)
    attn_gain = jnp.clip(1.0 + 0.18 * jax.random.normal(arg_keys[3], (N_SECTION, D), jnp.float32), 0.099609375, 1.8984375).astype(jnp.bfloat16)
    w_qkv = scatter_about(arg_keys[4], (N_SECTION, D, QKV), D ** -0.5, 0.1875, ((0, 2), (1, 4)))
    w_out = scatter_about(arg_keys[5], (N_SECTION, QDIM, D), (max(QDIM * 2 // SEQ, 1)) ** -0.5, 6.0, ((0, 2), (1, 4)))
    mlp_gain = jnp.clip(1.0 + 0.18 * jax.random.normal(arg_keys[6], (N_SECTION, D), jnp.float32), 0.099609375, 1.8984375).astype(jnp.bfloat16)
    w_gate = scatter_about(arg_keys[7], (N_SECTION, D, FF), D ** -0.5, 0.1875, ((0, 2), (1, 4)))
    w_up = scatter_about(arg_keys[8], (N_SECTION, D, FF), D ** -0.5, 0.1875, ((0, 2), (1, 4)))
    w_down = scatter_about(arg_keys[9], (N_SECTION, FF, D), FF ** -0.5, 0.125, ((0, 2), (1, 4)))
    return dict(block_input=block_input, out_cotangent=out_cotangent, block_table=block_table, attn_gain=attn_gain, w_qkv=w_qkv, w_out=w_out, mlp_gain=mlp_gain, w_gate=w_gate, w_up=w_up, w_down=w_down)


EPSILON = 1e-05
ROPE_BASE = 100000.0
MASKED = -1e+30
PRECISE = lax.Precision.HIGHEST

@jax.custom_vjp
def low(v):
    return lax.optimization_barrier(v.astype(jnp.bfloat16)).astype(jnp.float32)

@jax.custom_vjp
def low_back(v):
    return v

def low_keep(v):
    return (low(v), None)

def low_pass(kept, grad):
    return (grad,)

def back_keep(v):
    return (v, None)

def back_low(kept, grad):
    return (low(grad),)
low.defvjp(low_keep, low_pass)
low_back.defvjp(back_keep, back_low)

def rotary_tables(positions):
    half_size = HD // 2
    inverse = ROPE_BASE ** (-(jnp.arange(half_size, dtype=jnp.float32) * 2.0) / HD)
    angles = positions.astype(jnp.float32)[:, None] * inverse[None, :]
    return (jnp.cos(angles), jnp.sin(angles))

def rotate(values, cos_table, sin_table):
    half_size = values.shape[-1] // 2
    front_half = values[..., :half_size]
    back_half = values[..., half_size:]
    cos_wide = cos_table[:, None, :]
    sin_wide = sin_table[:, None, :]
    return jnp.concatenate([front_half * cos_wide - back_half * sin_wide, back_half * cos_wide + front_half * sin_wide], axis=-1)

def attention(queries, key_rot, values, positions):
    group_size = H // KVH
    block_rows = math.gcd(SEQ, 512)
    block_count = SEQ // block_rows
    query_blocks = queries.reshape(block_count, block_rows, KVH, group_size, HD)
    pos_blocks = positions.reshape(block_count, block_rows)

    def one_block(inputs):
        query_block, pos_block = inputs
        raw_scores = jnp.einsum('tkgd,skd->kgts', query_block, key_rot, precision=PRECISE) * HD ** (-0.5)
        raw_scores = low_back(raw_scores)
        allowed = positions[None, None, None, :] <= pos_block[None, None, :, None]
        raw_scores = jnp.where(allowed, raw_scores, MASKED)
        probabilities = low(jax.nn.softmax(raw_scores, axis=-1))
        return jnp.einsum('kgts,skd->tkgd', probabilities, values, precision=PRECISE)
    combined = lax.map(jax.checkpoint(one_block), (query_blocks, pos_blocks))
    return combined.reshape(SEQ, H * HD)

def layer(inflow, params, cos_table, sin_table, positions):
    gain_one, qkv_weight, out_weight, gain_two, gate_weight, up_weight, down_weight = params
    query_width = H * HD
    kv_width = KVH * HD
    residual = low_back(inflow)
    normed = low(residual * lax.rsqrt(lax.optimization_barrier(jnp.mean(residual * residual, axis=-1, keepdims=True)) + EPSILON) * gain_one)
    mixed_proj = low_back(jnp.dot(normed, qkv_weight, precision=PRECISE))
    queries = low(rotate(mixed_proj[:, :query_width].reshape(SEQ, H, HD), cos_table, sin_table))
    key_rot = low(rotate(mixed_proj[:, query_width:query_width + kv_width].reshape(SEQ, KVH, HD), cos_table, sin_table))
    values = low(mixed_proj[:, query_width + kv_width:].reshape(SEQ, KVH, HD))
    attended = attention(queries.reshape(SEQ, KVH, H // KVH, HD), key_rot, values, positions)
    attended = low(low_back(attended))
    middle = residual + low_back(jnp.dot(attended, out_weight, precision=PRECISE))
    second = low(middle * lax.rsqrt(lax.optimization_barrier(jnp.mean(middle * middle, axis=-1, keepdims=True)) + EPSILON) * gain_two)
    gate_proj = low_back(jnp.dot(second, gate_weight, precision=PRECISE))
    up_proj = low_back(jnp.dot(second, up_weight, precision=PRECISE))
    hidden = low(jax.nn.silu(gate_proj) * up_proj)
    return low(middle + low_back(jnp.dot(hidden, down_weight, precision=PRECISE)))

def reference(block_input, out_cotangent, block_table, attn_gain, w_qkv, w_out, mlp_gain, w_gate, w_up, w_down):
    half_rows = SEQ // BLOCKS
    positions = (jnp.repeat(block_table, half_rows) * half_rows + jnp.tile(jnp.arange(half_rows, dtype=jnp.int32), BLOCKS)).astype(jnp.int32)
    cos_table, sin_table = rotary_tables(positions)
    arrays = (attn_gain, w_qkv, w_out, mlp_gain, w_gate, w_up, w_down)
    weights = [tuple((array[section_pos].astype(jnp.float32) for array in arrays)) for section_pos in range(N_SECTION)]
    zero_grads = tuple((jnp.zeros(array.shape, jnp.float32) for array in weights[0]))

    def apply_layer(inflow, params):
        return layer(inflow, params, cos_table, sin_table, positions)

    def one_micro(totals, inputs):
        inflow, cotangent = inputs
        layer_outs = []
        pullbacks = []
        current = inflow.astype(jnp.float32)
        for section_pos in range(N_SECTION):
            current, pullback = jax.vjp(apply_layer, current, weights[section_pos])
            layer_outs.append(current)
            pullbacks.append(pullback)
        gradient = cotangent.astype(jnp.float32)
        input_list = [None] * N_SECTION
        new_totals = list(totals)
        for section_pos in reversed(range(N_SECTION)):
            gradient, param_grads = pullbacks[section_pos](gradient)
            input_list[section_pos] = gradient
            new_totals[section_pos] = tuple((left_sum + right_sum for left_sum, right_sum in zip(totals[section_pos], param_grads)))
        return (tuple(new_totals), (jnp.stack(layer_outs), jnp.stack(input_list)))
    initial = tuple((zero_grads for section_pos in range(N_SECTION)))
    totals, (layer_outs, input_list) = lax.scan(one_micro, initial, (block_input, out_cotangent))
    layer_outputs = jnp.transpose(layer_outs, (1, 0, 2, 3)).astype(jnp.bfloat16)
    input_grads = jnp.transpose(input_list, (1, 0, 2, 3)).astype(jnp.bfloat16)
    stacked = [jnp.stack([totals[section_pos][member] for section_pos in range(N_SECTION)]) for member in range(7)]
    return (layer_outputs, input_grads, stacked[0], stacked[1], stacked[2], stacked[3], stacked[4], stacked[5], stacked[6])
```

```python
import functools

import jax
import jax.numpy as jnp
from jax import lax
from jax.experimental import pallas as pl
from jax.experimental.pallas import tpu as pltpu
from jax.sharding import PartitionSpec as P

H = 15
KVH = 5
HD = 64
GROUP = H // KVH
QW = H * HD
KW = KVH * HD
LANES = 128
KEY_CHUNK = 512

EPSILON = 1e-05
ROPE_BASE = 100000.0
MASKED = -1e30
SCALE = HD**-0.5
F32 = jnp.float32
BF16 = jnp.bfloat16

WHOLE = pl.BlockSpec(memory_space=pltpu.VMEM)
SCALARS = pl.BlockSpec(memory_space=pltpu.SMEM)


def params(mib):
    return pltpu.CompilerParams(vmem_limit_bytes=mib * 1024 * 1024)


def cost(flops, moved, special=0):
    return pl.CostEstimate(flops=flops, bytes_accessed=moved, transcendentals=special)


def dot_nn(a, b):
    return lax.dot_general(a, b, (((1,), (0,)), ((), ())), preferred_element_type=F32)


def dot_nt(a, b):
    return lax.dot_general(a, b, (((1,), (1,)), ((), ())), preferred_element_type=F32)


def dot_tn(a, b):
    return lax.dot_general(a, b, (((0,), (0,)), ((), ())), preferred_element_type=F32)


def lane_of(shape):
    return lax.broadcasted_iota(jnp.int32, shape, 1)


def swap_halves(block, lane):
    ahead = pltpu.roll(block, LANES - HD // 2, 1)
    behind = pltpu.roll(block, HD // 2, 1)
    return jnp.where(lane % HD < HD // 2, ahead, behind)


def assemble_kernel(index_ref, *refs, shard_rows, step):
    out_ref = refs[-1]
    mine, other = refs[:-2], refs[-2]
    wa, section = index_ref[0], index_ref[1]
    rows = mine[0].shape[0]
    for k, piece in enumerate(mine):
        base = (wa ^ k) * shard_rows
        start = pl.multiple_of(base + section * step, 16)
        out_ref[pl.ds(start, rows), :] = piece[...]
        start = pl.multiple_of(base + (1 - section) * step, 16)
        out_ref[pl.ds(start, rows), :] = other[k]


def assemble(index, mine, other, shard_rows, step):
    width = mine[0].shape[1]
    total = shard_rows * len(mine)
    return pl.pallas_call(
        functools.partial(assemble_kernel, shard_rows=shard_rows, step=step),
        out_shape=jax.ShapeDtypeStruct((total, width), BF16),
        in_specs=[SCALARS] + [WHOLE] * (len(mine) + 1),
        out_specs=WHOLE,
        compiler_params=params(24),
        cost_estimate=cost(0, total * width * 6),
        name="assemble",
    )(index, *mine, other)


def pair_kernel(index_ref, *refs, shard_rows):
    out_ref = refs[-1]
    mine, other = refs[:-2], refs[-2]
    wa, section = index_ref[0], index_ref[1]
    rows, width = mine[0].shape
    left = pl.multiple_of(section * width, LANES)
    right = pl.multiple_of((1 - section) * width, LANES)
    for k, piece in enumerate(mine):
        start = pl.multiple_of((wa ^ k) * shard_rows, 16)
        out_ref[pl.ds(start, rows), pl.ds(left, width)] = piece[...]
        out_ref[pl.ds(start, rows), pl.ds(right, width)] = other[k]


def assemble_pair(index, mine, other):
    shard_rows, width = mine[0].shape
    total = shard_rows * len(mine)
    return pl.pallas_call(
        functools.partial(pair_kernel, shard_rows=shard_rows),
        out_shape=jax.ShapeDtypeStruct((total, 2 * width), BF16),
        in_specs=[SCALARS] + [WHOLE] * (len(mine) + 1),
        out_specs=WHOLE,
        compiler_params=params(24),
        cost_estimate=cost(0, total * width * 8),
        name="assemble_pair",
    )(index, *mine, other)


def project_kernel(u_ref, gain_ref, w_ref, cos_ref, sin_ref, normed_ref, q_ref, kv_ref, mixed_ref):
    u = u_ref[...].astype(F32)
    scale = lax.rsqrt(jnp.mean(u * u, axis=-1, keepdims=True) + EPSILON)
    normed = (u * scale * gain_ref[...].astype(F32)).astype(BF16)
    normed_ref[...] = normed
    mixed_ref[:, : w_ref.shape[1]] = dot_nn(normed, w_ref[...])
    cosine, sine = cos_ref[...], sin_ref[...]
    lane = lane_of(cosine.shape)
    low = lane < HD
    roped = {}

    def unit(h, high):
        j = h // 2
        if j not in roped:
            block = mixed_ref[:, j * LANES : (j + 1) * LANES]
            if h < H + KVH:
                block = block * cosine + swap_halves(block, lane) * sine
            roped[j] = block
        return roped[j] if (h % 2 == 1) == high else pltpu.roll(roped[j], HD, 1)

    for h in range(H):
        padded = jnp.where(low, unit(h, False) * SCALE, 0.0)
        q_ref[:, h * LANES : (h + 1) * LANES] = padded.astype(BF16)
    for g in range(KVH):
        both = jnp.where(low, unit(H + g, False), unit(H + KVH + g, True))
        kv_ref[:, g * LANES : (g + 1) * LANES] = both.astype(BF16)


def project(u, gain, weight, cosine, sine):
    rows, width = u.shape
    columns = weight.shape[1]
    padded = -(-columns // LANES) * LANES
    return pl.pallas_call(
        project_kernel,
        out_shape=(
            jax.ShapeDtypeStruct((rows, width), BF16),
            jax.ShapeDtypeStruct((rows, H * LANES), BF16),
            jax.ShapeDtypeStruct((rows, KVH * LANES), BF16),
        ),
        in_specs=[WHOLE] * 5,
        out_specs=(WHOLE,) * 3,
        scratch_shapes=[pltpu.VMEM((rows, padded), F32)],
        compiler_params=params(24),
        cost_estimate=cost(2 * rows * width * columns, width * columns * 2),
        name="project",
    )(u, gain, weight, cosine, sine)


def stack_heads(ref):
    return jnp.concatenate(
        [ref[:, i * LANES : (i + 1) * LANES] for i in range(GROUP)], axis=0
    )


def attend_kernel(qpos_ref, kpos_ref, q_ref, *refs):
    kv_refs, out_ref = refs[:-1], refs[-1]
    queries = stack_heads(q_ref)
    qpos = jnp.concatenate([qpos_ref[...]] * GROUP, axis=0)
    rows = queries.shape[0]
    top = jnp.full((rows, 1), MASKED, F32)
    total = jnp.zeros((rows, 1), F32)
    acc = jnp.zeros((rows, LANES), F32)
    for k, kv_ref in enumerate(kv_refs):
        for start in range(0, kv_ref.shape[0], KEY_CHUNK):
            size = min(KEY_CHUNK, kv_ref.shape[0] - start)
            kv = kv_ref[start : start + size, :]
            kpos = kpos_ref[k : k + 1, start : start + size]
            scores = jnp.where(kpos <= qpos, dot_nt(queries, kv), MASKED)
            new_top = jnp.maximum(top, jnp.max(scores, axis=-1, keepdims=True))
            fresh = jnp.exp(scores - new_top)
            decay = jnp.exp(top - new_top)
            total = total * decay + jnp.sum(fresh, axis=-1, keepdims=True)
            acc = acc * decay + dot_nn(fresh.astype(BF16), kv)
            top = new_top
    lse = top + jnp.log(total)
    out_ref[...] = jnp.where(lane_of(acc.shape) < HD, lse, acc / total)


def attend(qpos, kpos, queries, groups):
    rows = queries.shape[0]
    keys = groups[0].shape[0]
    pairs = H * rows * keys * len(groups)
    return pl.pallas_call(
        attend_kernel,
        out_shape=jax.ShapeDtypeStruct((H * rows, LANES), F32),
        grid=(KVH,),
        in_specs=[
            pl.BlockSpec((rows, 1), lambda g: (0, 0)),
            pl.BlockSpec(kpos.shape, lambda g: (0, 0)),
            pl.BlockSpec((rows, GROUP * LANES), lambda g: (0, g)),
        ]
        + [pl.BlockSpec((keys, LANES), lambda g: (0, g)) for _ in groups],
        out_specs=pl.BlockSpec((GROUP * rows, LANES), lambda g: (g, 0)),
        compiler_params=params(40),
        cost_estimate=cost(pairs * 512, keys * len(groups) * KVH * 256, pairs),
        name="attend",
    )(qpos, kpos, queries, *groups)


def attend_back_kernel(qpos_ref, kpos_ref, q_ref, g_ref, o_ref, *refs):
    count = (len(refs) - 1) // 2
    kv_refs, dq_ref, dkv_refs = refs[:count], refs[count], refs[count + 1 :]
    queries = stack_heads(q_ref)
    grads = stack_heads(g_ref)
    saved = o_ref[...]
    lse = jnp.transpose(saved)[0:1, :]
    delta = jnp.sum(jnp.transpose(grads.astype(F32) * saved), axis=0, keepdims=True)
    qpos = jnp.concatenate([qpos_ref[...]] * GROUP, axis=1)
    rows = queries.shape[0]
    acc = jnp.zeros((rows, LANES), F32)
    for k, kv_ref in enumerate(kv_refs):
        for start in range(0, kv_ref.shape[0], KEY_CHUNK):
            size = min(KEY_CHUNK, kv_ref.shape[0] - start)
            kv = kv_ref[start : start + size, :]
            kpos = kpos_ref[start : start + size, k : k + 1]
            scores = jnp.where(kpos <= qpos, dot_nt(kv, queries), MASKED)
            probs = jnp.exp(scores - lse)
            grad_probs = dot_nt(kv, grads)
            grad_scores = (probs * (grad_probs - delta)).astype(BF16)
            acc = acc + dot_tn(grad_scores, kv)
            dkv = dot_nn(grad_scores, queries) + dot_nn(probs.astype(BF16), grads)
            dkv_refs[k][start : start + size, :] = dkv.astype(BF16)
    tok = q_ref.shape[0]
    for i in range(GROUP):
        dq_ref[:, i * LANES : (i + 1) * LANES] = acc[i * tok : (i + 1) * tok] * SCALE


def attend_back(qpos_row, kpos_column, queries, grads, saved, groups):
    rows = queries.shape[0]
    keys = groups[0].shape[0]
    pairs = H * rows * keys * len(groups)
    heads = pl.BlockSpec((rows, GROUP * LANES), lambda g: (0, g))
    kv_block = pl.BlockSpec((keys, LANES), lambda g: (0, g))
    result = pl.pallas_call(
        attend_back_kernel,
        out_shape=(jax.ShapeDtypeStruct((rows, H * LANES), F32),)
        + tuple(jax.ShapeDtypeStruct(group.shape, BF16) for group in groups),
        grid=(KVH,),
        in_specs=[
            pl.BlockSpec((1, rows), lambda g: (0, 0)),
            pl.BlockSpec(kpos_column.shape, lambda g: (0, 0)),
            heads,
            heads,
            pl.BlockSpec((GROUP * rows, LANES), lambda g: (g, 0)),
        ]
        + [kv_block for _ in groups],
        out_specs=(heads,) + tuple(kv_block for _ in groups),
        compiler_params=params(40),
        cost_estimate=cost(pairs * 1280, keys * len(groups) * KVH * 512, pairs),
        name="attend_back",
    )(qpos_row, kpos_column, queries, grads, saved, *groups)
    return result[0], result[1:]


def close_kernel(u_ref, saved_ref, w_ref, gain_ref, low_ref, middle_ref, second_ref):
    rows = u_ref.shape[0]
    lane = lane_of((rows, LANES))
    for j in range(H // 2):
        even = pltpu.roll(saved_ref[2 * j * rows : (2 * j + 1) * rows, :], HD, 1)
        odd = saved_ref[(2 * j + 1) * rows : (2 * j + 2) * rows, :]
        low_ref[:, j * LANES : (j + 1) * LANES] = jnp.where(lane < HD, even, odd).astype(BF16)
    last = pltpu.roll(saved_ref[(H - 1) * rows : H * rows, :], HD, 1)
    low_ref[:, (H - 1) * HD : H * HD] = last[:, :HD].astype(BF16)
    middle = u_ref[...].astype(F32) + dot_nn(low_ref[...], w_ref[...])
    middle_ref[...] = middle
    scale = lax.rsqrt(jnp.mean(middle * middle, axis=-1, keepdims=True) + EPSILON)
    second_ref[...] = (middle * scale * gain_ref[...].astype(F32)).astype(BF16)


def close_attention(u, saved, weight, gain):
    rows, width = u.shape
    return pl.pallas_call(
        close_kernel,
        out_shape=(
            jax.ShapeDtypeStruct((rows, QW), BF16),
            jax.ShapeDtypeStruct((rows, width), F32),
            jax.ShapeDtypeStruct((rows, width), BF16),
        ),
        in_specs=[WHOLE] * 4,
        out_specs=(WHOLE,) * 3,
        compiler_params=params(24),
        cost_estimate=cost(2 * rows * QW * width, QW * width * 2),
        name="close_attention",
    )(u, saved, weight, gain)


def mlp_kernel(*refs, count):
    pieces, w_ref, down_ref = refs[:count], refs[count], refs[count + 1]
    wide_ref, hidden_ref = refs[count + 2 : count + 4]
    outs = refs[count + 4 :]
    rows = pieces[0].shape[0]
    second = jnp.concatenate([piece[...] for piece in pieces], axis=0)
    wide = dot_nn(second, w_ref[...])
    wide_ref[...] = wide
    half = wide.shape[1] // 2
    gate, up = wide[:, :half], wide[:, half:]
    hidden = (gate * jax.nn.sigmoid(gate) * up).astype(BF16)
    hidden_ref[...] = hidden
    partial = dot_nn(hidden, down_ref[...])
    for k, out in enumerate(outs):
        out[...] = partial[k * rows : (k + 1) * rows].astype(out.dtype)


def mlp(pieces, weight, down):
    count = len(pieces)
    rows, width = pieces[0].shape
    columns = weight.shape[1]
    result = pl.pallas_call(
        functools.partial(mlp_kernel, count=count),
        out_shape=(
            jax.ShapeDtypeStruct((count * rows, columns), F32),
            jax.ShapeDtypeStruct((count * rows, columns // 2), BF16),
            jax.ShapeDtypeStruct((rows, width), F32),
        )
        + tuple(jax.ShapeDtypeStruct((rows, width), BF16) for _ in range(count - 1)),
        in_specs=[WHOLE] * (count + 2),
        out_specs=(WHOLE,) * (count + 2),
        compiler_params=params(40),
        cost_estimate=cost(3 * count * rows * width * columns, width * columns * 8),
        name="mlp",
    )(*pieces, weight, down)
    return result[0], result[1], result[2:]


def mlp_back_kernel(*refs, count):
    pieces, wide_ref, w_ref, down_ref = refs[:count], *refs[count : count + 3]
    grads_ref, outs = refs[count + 3], refs[count + 4 :]
    rows = pieces[0].shape[0]
    grad_y = jnp.concatenate([piece[...] for piece in pieces], axis=0)
    grad_hidden = dot_nt(grad_y, down_ref[...])
    half = wide_ref.shape[1] // 2
    gate, up = wide_ref[:, :half], wide_ref[:, half:]
    sig = jax.nn.sigmoid(gate)
    grads_ref[:, :half] = (grad_hidden * up * sig * (1.0 + gate * (1.0 - sig))).astype(BF16)
    grads_ref[:, half:] = (grad_hidden * gate * sig).astype(BF16)
    partial = dot_nt(grads_ref[...], w_ref[...])
    for k, out in enumerate(outs):
        out[...] = partial[k * rows : (k + 1) * rows].astype(out.dtype)


def mlp_back(pieces, wide, weight, down):
    count = len(pieces)
    rows, width = pieces[0].shape
    columns = weight.shape[1]
    result = pl.pallas_call(
        functools.partial(mlp_back_kernel, count=count),
        out_shape=(
            jax.ShapeDtypeStruct((count * rows, columns), BF16),
            jax.ShapeDtypeStruct((rows, width), F32),
        )
        + tuple(jax.ShapeDtypeStruct((rows, width), BF16) for _ in range(count - 1)),
        in_specs=[WHOLE] * (count + 3),
        out_specs=(WHOLE,) * (count + 1),
        compiler_params=params(40),
        cost_estimate=cost(3 * count * rows * width * columns, width * columns * 8),
        name="mlp_back",
    )(*pieces, wide, weight, down)
    return result[0], result[1:]


def norm_back(values, gain, gradient):
    scaling = lax.rsqrt(jnp.mean(values * values, axis=-1, keepdims=True) + EPSILON)
    gain_grad = jnp.sum(gradient * values * scaling, axis=0, keepdims=True)
    scaled = gradient * gain.astype(F32)
    inner = jnp.mean(scaled * values, axis=-1, keepdims=True)
    return gain_grad, scaling * scaled - values * (scaling * scaling * scaling) * inner


def open_back_kernel(*refs, count):
    terms = refs[:count]
    middle_ref, gain_ref, y_ref, w_ref = refs[count : count + 4]
    grad_ref, low_ref, padded_ref, gain_grad_ref, wide_ref = refs[count + 4 :]
    gradient = terms[0][...]
    for term in terms[1:]:
        gradient = gradient + term[...].astype(F32)
    gain_grad, through = norm_back(middle_ref[...], gain_ref[...], gradient)
    gain_grad_ref[...] = gain_grad
    grad_middle = y_ref[...].astype(F32) + through
    grad_ref[...] = grad_middle
    low = grad_middle.astype(BF16)
    low_ref[...] = low
    wide_ref[:, :QW] = dot_nt(low, w_ref[...])
    lane = lane_of((low.shape[0], LANES))
    for h in range(H):
        block = wide_ref[:, h // 2 * LANES : (h // 2 + 1) * LANES]
        placed = block if h % 2 else pltpu.roll(block, HD, 1)
        padded_ref[:, h * LANES : (h + 1) * LANES] = jnp.where(lane < HD, 0.0, placed).astype(BF16)


def open_back(terms, middle, gain, grad_y, weight):
    rows, width = middle.shape
    count = len(terms)
    return pl.pallas_call(
        functools.partial(open_back_kernel, count=count),
        out_shape=(
            jax.ShapeDtypeStruct((rows, width), F32),
            jax.ShapeDtypeStruct((rows, width), BF16),
            jax.ShapeDtypeStruct((rows, H * LANES), BF16),
            jax.ShapeDtypeStruct((1, width), F32),
        ),
        in_specs=[WHOLE] * (count + 4),
        out_specs=(WHOLE,) * 4,
        scratch_shapes=[pltpu.VMEM((rows, (H + 1) // 2 * LANES), F32)],
        compiler_params=params(24),
        cost_estimate=cost(2 * rows * QW * width, QW * width * 2),
        name="open_back",
    )(*terms, middle, gain, grad_y, weight)


def project_back_kernel(*refs, count):
    terms = refs[:count]
    dq_ref, cos_ref, sin_ref, w_ref, u_ref, gain_ref, middle_ref = refs[count : count + 7]
    mixed_ref, out_ref, gain_grad_ref, wide_ref = refs[count + 7 :]
    grad_kv = terms[0][...].astype(F32)
    for term in terms[1:]:
        grad_kv = grad_kv + term[...].astype(F32)
    cosine, sine = cos_ref[...], sin_ref[...]
    lane = lane_of(cosine.shape)
    low = lane < HD

    def turned(block):
        return block * cosine - swap_halves(block, lane) * sine

    def unit(h, high):
        if h < H:
            block, at_high = turned(dq_ref[:, h * LANES : (h + 1) * LANES]), False
        elif h < H + KVH:
            g = h - H
            block, at_high = turned(grad_kv[:, g * LANES : (g + 1) * LANES]), False
        else:
            g = h - H - KVH
            block, at_high = grad_kv[:, g * LANES : (g + 1) * LANES], True
        return block if at_high == high else pltpu.roll(block, HD, 1)

    units = H + 2 * KVH
    for j in range((units + 1) // 2):
        block = unit(2 * j, False)
        if 2 * j + 1 < units:
            block = jnp.where(low, block, unit(2 * j + 1, True))
        wide_ref[:, j * LANES : (j + 1) * LANES] = block.astype(BF16)
    grad_mixed = wide_ref[:, : w_ref.shape[1]]
    mixed_ref[...] = grad_mixed
    gradient = dot_nt(grad_mixed, w_ref[...])
    gain_grad, through = norm_back(u_ref[...].astype(F32), gain_ref[...], gradient)
    gain_grad_ref[...] = gain_grad
    out_ref[...] = (middle_ref[...] + through).astype(BF16)


def project_back(terms, dq, cosine, sine, weight, u, gain, grad_middle):
    rows, width = u.shape
    columns = weight.shape[1]
    padded = -(-columns // LANES) * LANES
    count = len(terms)
    return pl.pallas_call(
        functools.partial(project_back_kernel, count=count),
        out_shape=(
            jax.ShapeDtypeStruct((rows, columns), BF16),
            jax.ShapeDtypeStruct((rows, width), BF16),
            jax.ShapeDtypeStruct((1, width), F32),
        ),
        in_specs=[WHOLE] * (count + 7),
        out_specs=(WHOLE,) * 3,
        scratch_shapes=[pltpu.VMEM((rows, padded), BF16)],
        compiler_params=params(24),
        cost_estimate=cost(2 * rows * width * columns, width * columns * 2),
        name="project_back",
    )(*terms, dq, cosine, sine, weight, u, gain, grad_middle)


def to_sibling(value):
    return lax.ppermute(value, "section", [(0, 1), (1, 0)])


def to_peer(value, k):
    count = lax.axis_size("wa")
    return lax.ppermute(value, "wa", [(i, i ^ k) for i in range(count)])


def gather_wa(value):
    return [value] + [to_peer(value, k) for k in range(1, lax.axis_size("wa"))]


def send_wa(pieces):
    return [pieces[0]] + [to_peer(piece, k) for k, piece in enumerate(pieces) if k]


def rotates(count):
    return count <= 4


def gather_ctx(value):
    count = lax.axis_size("ctx")
    if not rotates(count):
        return lax.all_gather(value, "ctx", axis=0, tiled=True)
    pieces = [value]
    for k in range(1, count):
        pieces.append(lax.ppermute(value, "ctx", [(i, (i + k) % count) for i in range(count)]))
    return jnp.concatenate(pieces, axis=0)


def scatter_ctx(value):
    count = lax.axis_size("ctx")
    rows = value.shape[0] // count
    if not rotates(count):
        blocks = value.reshape(count, rows, value.shape[1])
        return list(lax.all_to_all(blocks, "ctx", 0, 0, tiled=True))
    pieces = [value[:rows]]
    for k in range(1, count):
        piece = value[k * rows : (k + 1) * rows]
        pieces.append(lax.ppermute(piece, "ctx", [(i, (i - k) % count) for i in range(count)]))
    return pieces


def at(value, index, size, dim):
    return lax.dynamic_slice_in_dim(value, index * size, size, dim)


def added(terms):
    total = terms[0].astype(F32)
    for term in terms[1:]:
        total = total + term.astype(F32)
    return total


def per_device(
    block_input, out_cotangent, block_table, attn_gain, w_qkv, w_out, mlp_gain, w_gate, w_up, w_down
):
    section = lax.axis_index("section")
    wa = lax.axis_index("wa")
    ctx = lax.axis_index("ctx")
    wa_count = lax.axis_size("wa")
    ctx_count = lax.axis_size("ctx")
    layers = lax.axis_size("section")
    first = section == 0
    peers = range(wa_count)
    index = jnp.stack([wa, section]).astype(jnp.int32)
    micro_count, tok_rows, width = block_input.shape
    half_rows = tok_rows // 2
    shard_rows = w_qkv.shape[1]
    ff_part = w_down.shape[1]
    w_qkv, w_out, w_gate, w_up, w_down = (a[0] for a in (w_qkv, w_out, w_gate, w_up, w_down))

    in_block = jnp.arange(half_rows, dtype=jnp.int32)
    table = block_table.reshape(-1, 2)

    def positions_of(devices):
        return (table[devices][..., None] * half_rows + in_block).reshape(-1)

    own_pos = positions_of((ctx * wa_count + wa)[None])
    steps = jnp.arange(ctx_count)
    sources = (ctx - steps) % ctx_count if rotates(ctx_count) else steps
    key_pos = jnp.stack([positions_of(sources * wa_count + (wa ^ k)) for k in peers])
    key_pos_column = key_pos.T
    qpos_column, qpos_row = own_pos[:, None], own_pos[None, :]
    inverse = ROPE_BASE ** (-(jnp.arange(HD // 2, dtype=F32) * 2.0) / HD)
    angles = own_pos.astype(F32)[:, None] * inverse[None, :]
    cosine = jnp.tile(jnp.cos(angles), (1, 2 * LANES // HD))
    sines = jnp.sin(angles)
    sine = jnp.tile(jnp.concatenate([-sines, sines], axis=1), (1, LANES // HD))

    part_rows = shard_rows // 2 + 8
    part_step = shard_rows - part_rows

    def halves(shard):
        keep = lax.dynamic_slice_in_dim(shard, section * part_step, part_rows, 0)
        other = to_sibling(lax.dynamic_slice_in_dim(shard, (1 - section) * part_step, part_rows, 0))
        return jnp.where(first, keep, other), jnp.where(first, other, keep)

    def fetch_rows(part):
        mine = gather_wa(part)
        return assemble(index, mine, to_sibling(jnp.stack(mine)), shard_rows, part_step)

    def fetch_columns(part):
        mine = send_wa([at(part, wa ^ k, ff_part, 1) for k in peers])
        return assemble_pair(index, mine, to_sibling(jnp.stack(mine)))

    qkv_parts = halves(w_qkv)
    out_parts = halves(w_out)
    crossing = to_sibling(jnp.where(first, w_up, w_gate))
    wide_parts = (jnp.where(first, w_gate, crossing), jnp.where(first, crossing, w_up))
    down_other = to_sibling(w_down)
    downs = (jnp.where(first, w_down, down_other), jnp.where(first, down_other, w_down))
    gains = jnp.concatenate([attn_gain, mlp_gain], axis=0)
    gains = lax.all_gather(gains, ("section", "wa"), axis=0, tiled=False)
    gains = gains.reshape(layers, wa_count, 2, -1).transpose(0, 2, 1, 3).reshape(layers, 2, 1, -1)

    qkvs, outs, wides = [], [], []
    for layer in range(layers):
        qkvs.append(fetch_rows(qkv_parts[layer]))
        outs.append(fetch_rows(out_parts[layer]))
        wides.append(fetch_columns(wide_parts[layer]))

    u = lax.dynamic_index_in_dim(block_input, section, 0, keepdims=False)
    cotangent = lax.dynamic_index_in_dim(out_cotangent, section, 0, keepdims=False)
    records, results = [], []
    for layer in range(layers):
        normed, queries, kv = project(u, gains[layer, 0], qkvs[layer], cosine, sine)
        groups = gather_wa(gather_ctx(kv))
        saved = attend(qpos_column, key_pos, queries, groups)
        low, middle, second = close_attention(u, saved, outs[layer], gains[layer, 1])
        seconds = gather_wa(second)
        wide, hidden, partial = mlp(seconds, wides[layer], downs[layer])
        terms = send_wa(partial)
        result = (middle + added(terms)).astype(BF16)
        records.append((u, normed, queries, groups, saved, low, middle, seconds, wide, hidden))
        results.append(result)
        u = result

    gain_grads, input_grads, weight_grads = [None] * layers, [None] * layers, [None] * layers
    grad_y = cotangent
    for layer in reversed(range(layers)):
        u, normed, queries, groups, saved, low, middle, seconds, wide, hidden = records[layer]
        grad_ys = gather_wa(grad_y)
        grad_wide, partial = mlp_back(grad_ys, wide, wides[layer], downs[layer])
        terms = send_wa(partial)
        grad_middle, grad_low, grad_heads, gain_two_grad = open_back(
            terms, middle, gains[layer, 1], grad_y, outs[layer]
        )
        dq, dkv = attend_back(qpos_row, key_pos_column, queries, grad_heads, saved, groups)
        gathered = added(send_wa(list(dkv))).astype(BF16)
        terms = scatter_ctx(gathered)
        grad_mixed, grad_u, gain_one_grad = project_back(
            terms, dq, cosine, sine, qkvs[layer], u, gains[layer, 0], grad_middle
        )
        gain_grads[layer] = (gain_one_grad, gain_two_grad)
        input_grads[layer] = grad_u

        all_seconds = jnp.concatenate(seconds, axis=0)
        all_grads = jnp.concatenate(grad_ys, axis=0)
        wide_grad = dot_tn(all_seconds, grad_wide).astype(BF16)
        down_grad = dot_tn(hidden, all_grads).astype(BF16)
        out_grad = dot_tn(low, grad_low).astype(BF16)
        qkv_grad = dot_tn(normed, grad_mixed).astype(BF16)

        def over_cores(value, size, dim):
            keep = at(value, section, size, dim)
            other = to_sibling(at(value, 1 - section, size, dim))
            return (keep.astype(F32) + other.astype(F32)).astype(BF16)

        wide_half = over_cores(wide_grad, ff_part, 1)
        pieces = send_wa([at(wide_half, wa ^ k, shard_rows, 0) for k in peers])
        wide_rows = jnp.zeros((shard_rows, wa_count * ff_part), BF16)
        for k in peers:
            wide_rows = lax.dynamic_update_slice_in_dim(
                wide_rows, pieces[k], (wa ^ k) * ff_part, 1
            )
        down_half = over_cores(down_grad, ff_part // 2, 0)

        def rows_over_wa(value):
            columns = value.shape[1]
            blocks = value.reshape(wa_count, 2, shard_rows // 2, columns)
            half = over_cores(blocks, 1, 1)[:, 0]
            pieces = send_wa([at(half, wa ^ k, 1, 0)[0] for k in peers])
            return added(pieces).astype(BF16)

        out_half = rows_over_wa(out_grad)
        qkv_half = rows_over_wa(qkv_grad)
        wide_rows, down_half = lax.psum((wide_rows, down_half), "ctx")
        out_half, qkv_half = lax.psum((out_half, qkv_half), "ctx")
        weight_grads[layer] = (wide_rows, down_half, out_half, qkv_half)
        grad_y = grad_u

    def by_layer(values):
        mine = jnp.where(first, values[0], values[1])
        other = to_sibling(jnp.where(first, values[1], values[0]))
        return jnp.where(first, mine, other), jnp.where(first, other, mine)

    def both(values):
        return jnp.stack(by_layer(values))[None]

    def joined(position):
        parts = by_layer([weight_grads[layer][position] for layer in range(layers)])
        return jnp.concatenate(parts, axis=0).astype(F32)[None]

    gate_grad, up_grad = by_layer([weight_grads[layer][0] for layer in range(layers)])
    gain_sums = lax.psum(
        jnp.concatenate([jnp.concatenate(pair, axis=0) for pair in gain_grads], axis=0),
        ("section", "ctx", "wa"),
    ).reshape(layers, 2, width)
    own_gains = at(lax.dynamic_index_in_dim(gain_sums, section, 0), wa, shard_rows, 2)
    return (
        both(results),
        both(input_grads),
        own_gains[:, 0],
        joined(3),
        joined(2),
        own_gains[:, 1],
        gate_grad.astype(F32)[None],
        up_grad.astype(F32)[None],
        joined(1),
    )


def solution(mesh):
    return jax.shard_map(
        per_device,
        mesh=mesh,
        in_specs=(
            P(None, ("ctx", "wa"), None),
            P(None, ("ctx", "wa"), None),
            P(),
            P("section", "wa"),
            P("section", "wa", None),
            P("section", "wa", None),
            P("section", "wa"),
            P("section", "wa", None),
            P("section", "wa", None),
            P("section", "wa", None),
        ),
        out_specs=(
            P("section", None, ("ctx", "wa"), None),
            P("section", None, ("ctx", "wa"), None),
            P("section", "wa"),
            P("section", "wa", None),
            P("section", "wa", None),
            P("section", "wa"),
            P("section", "wa", None),
            P("section", "wa", None),
            P("section", "wa", None),
        ),
        check_vma=False,
    )
```

```python
import functools

import jax
import jax.numpy as jnp
from jax import lax
from jax.experimental import pallas as pl
from jax.experimental.pallas import tpu as pltpu
from jax.sharding import PartitionSpec as P

H = 15
KVH = 5
HD = 64
GROUP = H // KVH
QW = H * HD
KW = KVH * HD
LANES = 128
KEY_CHUNK = 512

EPSILON = 1e-05
ROPE_BASE = 100000.0
MASKED = -1e30
SCALE = HD**-0.5
F32 = jnp.float32
BF16 = jnp.bfloat16

WHOLE = pl.BlockSpec(memory_space=pltpu.VMEM)
SCALARS = pl.BlockSpec(memory_space=pltpu.SMEM)


def params(mib):
    return pltpu.CompilerParams(vmem_limit_bytes=mib * 1024 * 1024)


def cost(us):
    return pl.CostEstimate(flops=int(us * 1.15e9), bytes_accessed=0, transcendentals=0)


def dot_nn(a, b):
    return lax.dot_general(a, b, (((1,), (0,)), ((), ())), preferred_element_type=F32)


def dot_nt(a, b):
    return lax.dot_general(a, b, (((1,), (1,)), ((), ())), preferred_element_type=F32)


def dot_tn(a, b):
    return lax.dot_general(a, b, (((0,), (0,)), ((), ())), preferred_element_type=F32)


def lane_of(shape):
    return lax.broadcasted_iota(jnp.int32, shape, 1)


def swap_halves(block, lane):
    ahead = pltpu.roll(block, LANES - HD // 2, 1)
    behind = pltpu.roll(block, HD // 2, 1)
    return jnp.where(lane % HD < HD // 2, ahead, behind)


def join_kernel(*refs):
    pieces, out_ref = refs[:-1], refs[-1]
    rows = pieces[0].shape[0]
    for k, piece in enumerate(pieces):
        out_ref[k * rows : (k + 1) * rows, :] = piece[...]


def join(pieces):
    rows, width = pieces[0].shape
    return pl.pallas_call(
        join_kernel,
        out_shape=jax.ShapeDtypeStruct((rows * len(pieces), width), pieces[0].dtype),
        in_specs=[WHOLE] * len(pieces),
        out_specs=WHOLE,
        compiler_params=params(24),
        cost_estimate=cost(1),
        name="join",
    )(*pieces)


def assemble_kernel(index_ref, mine_ref, other_ref, out_ref, *, relative, rows, shard_rows, step):
    wa, section = index_ref[0], index_ref[1]
    count = out_ref.shape[0] // shard_rows
    part = mine_ref.shape[0] // count
    for k in range(count):
        base = ((wa ^ k) if relative else k) * shard_rows
        start = pl.multiple_of(base + section * step, 16)
        out_ref[pl.ds(start, rows), :] = mine_ref[k * part : k * part + rows, :]
        start = pl.multiple_of(base + (1 - section) * step, 16)
        out_ref[pl.ds(start, rows), :] = other_ref[k * part : k * part + rows, :]


def assemble(index, mine, other, count, relative, rows, shard_rows, step):
    width = mine.shape[1]
    total = shard_rows * count
    return pl.pallas_call(
        functools.partial(
            assemble_kernel, relative=relative, rows=rows, shard_rows=shard_rows, step=step
        ),
        out_shape=jax.ShapeDtypeStruct((total, width), BF16),
        in_specs=[SCALARS, WHOLE, WHOLE],
        out_specs=WHOLE,
        compiler_params=params(24),
        cost_estimate=cost(2),
        name="assemble",
    )(index, mine, other)


def pair_kernel(index_ref, mine_ref, other_ref, out_ref, *, shard_rows):
    wa, section = index_ref[0], index_ref[1]
    width = mine_ref.shape[1]
    left = pl.multiple_of(section * width, LANES)
    right = pl.multiple_of((1 - section) * width, LANES)
    for k in range(out_ref.shape[0] // shard_rows):
        rows = pl.ds(pl.multiple_of((wa ^ k) * shard_rows, 16), shard_rows)
        piece = slice(k * shard_rows, (k + 1) * shard_rows)
        out_ref[rows, pl.ds(left, width)] = mine_ref[piece, :]
        out_ref[rows, pl.ds(right, width)] = other_ref[piece, :]


def assemble_pair(index, mine, other, shard_rows):
    total, width = mine.shape
    return pl.pallas_call(
        functools.partial(pair_kernel, shard_rows=shard_rows),
        out_shape=jax.ShapeDtypeStruct((total, 2 * width), BF16),
        in_specs=[SCALARS, WHOLE, WHOLE],
        out_specs=WHOLE,
        compiler_params=params(24),
        cost_estimate=cost(2.4),
        name="assemble_pair",
    )(index, mine, other)


def project_kernel(*refs, count):
    terms, refs = refs[:count], refs[count:]
    gain_ref, w_ref, cos_ref, sin_ref, u_ref, normed_ref, q_ref, kv_ref, mixed_ref = refs
    u = terms[0][...].astype(F32)
    for term in terms[1:]:
        u = u + term[...].astype(F32)
    u_ref[...] = u.astype(BF16)
    u = u_ref[...].astype(F32)
    scale = lax.rsqrt(jnp.mean(u * u, axis=-1, keepdims=True) + EPSILON)
    normed = (u * scale * gain_ref[...].astype(F32)).astype(BF16)
    normed_ref[...] = normed
    mixed_ref[:, : w_ref.shape[1]] = dot_nn(normed, w_ref[...])
    cosine, sine = cos_ref[...], sin_ref[...]
    lane = lane_of(cosine.shape)
    low = lane < HD
    roped = {}

    def unit(h, high):
        j = h // 2
        if j not in roped:
            block = mixed_ref[:, j * LANES : (j + 1) * LANES]
            if h < H + KVH:
                block = block * cosine + swap_halves(block, lane) * sine
            roped[j] = block
        return roped[j] if (h % 2 == 1) == high else pltpu.roll(roped[j], HD, 1)

    for h in range(H):
        padded = jnp.where(low, unit(h, False) * SCALE, 0.0)
        q_ref[:, h * LANES : (h + 1) * LANES] = padded.astype(BF16)
    for g in range(KVH):
        both = jnp.where(low, unit(H + g, False), unit(H + KVH + g, True))
        kv_ref[:, g * LANES : (g + 1) * LANES] = both.astype(BF16)


def project(terms, gain, weight, cosine, sine):
    rows, width = terms[0].shape
    count = len(terms)
    columns = weight.shape[1]
    padded = -(-columns // LANES) * LANES
    return pl.pallas_call(
        functools.partial(project_kernel, count=count),
        out_shape=(
            jax.ShapeDtypeStruct((rows, width), BF16),
            jax.ShapeDtypeStruct((rows, width), BF16),
            jax.ShapeDtypeStruct((rows, H * LANES), BF16),
            jax.ShapeDtypeStruct((rows, KVH * LANES), BF16),
        ),
        in_specs=[WHOLE] * (count + 4),
        out_specs=(WHOLE,) * 4,
        scratch_shapes=[pltpu.VMEM((rows, padded), F32)],
        compiler_params=params(24),
        cost_estimate=cost(2),
        name="project",
    )(*terms, gain, weight, cosine, sine)


def stack_heads(ref):
    return jnp.concatenate(
        [ref[:, i * LANES : (i + 1) * LANES] for i in range(GROUP)], axis=0
    )


def attend_kernel(qpos_ref, kpos_ref, q_ref, *refs):
    kv_refs, out_ref = refs[:-1], refs[-1]
    queries = stack_heads(q_ref)
    qpos = jnp.concatenate([qpos_ref[...]] * GROUP, axis=0)
    rows = queries.shape[0]
    top = jnp.full((rows, 1), MASKED, F32)
    total = jnp.zeros((rows, 1), F32)
    acc = jnp.zeros((rows, LANES), F32)
    for k, kv_ref in enumerate(kv_refs):
        for start in range(0, kv_ref.shape[0], KEY_CHUNK):
            size = min(KEY_CHUNK, kv_ref.shape[0] - start)
            kv = kv_ref[start : start + size, :]
            kpos = kpos_ref[k : k + 1, start : start + size]
            scores = jnp.where(kpos <= qpos, dot_nt(queries, kv), MASKED)
            new_top = jnp.maximum(top, jnp.max(scores, axis=-1, keepdims=True))
            fresh = jnp.exp(scores - new_top)
            decay = jnp.exp(top - new_top)
            total = total * decay + jnp.sum(fresh, axis=-1, keepdims=True)
            acc = acc * decay + dot_nn(fresh.astype(BF16), kv)
            top = new_top
    lse = top + jnp.log(total)
    out_ref[...] = jnp.where(lane_of(acc.shape) < HD, lse, acc / total)


def attend(qpos, kpos, queries, groups):
    rows = queries.shape[0]
    keys = groups[0].shape[0]
    pairs = H * rows * keys * len(groups)
    return pl.pallas_call(
        attend_kernel,
        out_shape=jax.ShapeDtypeStruct((H * rows, LANES), F32),
        grid=(KVH,),
        in_specs=[
            pl.BlockSpec((rows, 1), lambda g: (0, 0)),
            pl.BlockSpec(kpos.shape, lambda g: (0, 0)),
            pl.BlockSpec((rows, GROUP * LANES), lambda g: (0, g)),
        ]
        + [pl.BlockSpec((keys, LANES), lambda g: (0, g)) for _ in groups],
        out_specs=pl.BlockSpec((GROUP * rows, LANES), lambda g: (g, 0)),
        compiler_params=params(40),
        cost_estimate=cost(9.6),
        name="attend",
    )(qpos, kpos, queries, *groups)


def attend_back_kernel(qpos_ref, kpos_ref, q_ref, g_ref, o_ref, *refs):
    count = (len(refs) - 1) // 2
    kv_refs, dq_ref, dkv_refs = refs[:count], refs[count], refs[count + 1 :]
    queries = stack_heads(q_ref)
    grads = stack_heads(g_ref)
    saved = o_ref[...]
    lse = jnp.transpose(saved)[0:1, :]
    delta = jnp.sum(jnp.transpose(grads.astype(F32) * saved), axis=0, keepdims=True)
    qpos = jnp.concatenate([qpos_ref[...]] * GROUP, axis=1)
    rows = queries.shape[0]
    acc = jnp.zeros((rows, LANES), F32)
    for k, kv_ref in enumerate(kv_refs):
        for start in range(0, kv_ref.shape[0], KEY_CHUNK):
            size = min(KEY_CHUNK, kv_ref.shape[0] - start)
            kv = kv_ref[start : start + size, :]
            kpos = kpos_ref[start : start + size, k : k + 1]
            scores = jnp.where(kpos <= qpos, dot_nt(kv, queries), MASKED)
            probs = jnp.exp(scores - lse)
            grad_probs = dot_nt(kv, grads)
            grad_scores = (probs * (grad_probs - delta)).astype(BF16)
            acc = acc + dot_tn(grad_scores, kv)
            dkv = dot_nn(grad_scores, queries) + dot_nn(probs.astype(BF16), grads)
            dkv_refs[k][start : start + size, :] = dkv.astype(BF16)
    tok = q_ref.shape[0]
    for i in range(GROUP):
        dq_ref[:, i * LANES : (i + 1) * LANES] = acc[i * tok : (i + 1) * tok] * SCALE


def attend_back(qpos_row, kpos_column, queries, grads, saved, groups):
    rows = queries.shape[0]
    keys = groups[0].shape[0]
    pairs = H * rows * keys * len(groups)
    heads = pl.BlockSpec((rows, GROUP * LANES), lambda g: (0, g))
    kv_block = pl.BlockSpec((keys, LANES), lambda g: (0, g))
    result = pl.pallas_call(
        attend_back_kernel,
        out_shape=(jax.ShapeDtypeStruct((rows, H * LANES), F32),)
        + tuple(jax.ShapeDtypeStruct(group.shape, BF16) for group in groups),
        grid=(KVH,),
        in_specs=[
            pl.BlockSpec((1, rows), lambda g: (0, 0)),
            pl.BlockSpec(kpos_column.shape, lambda g: (0, 0)),
            heads,
            heads,
            pl.BlockSpec((GROUP * rows, LANES), lambda g: (g, 0)),
        ]
        + [kv_block for _ in groups],
        out_specs=(heads,) + tuple(kv_block for _ in groups),
        compiler_params=params(40),
        cost_estimate=cost(15.2),
        name="attend_back",
    )(qpos_row, kpos_column, queries, grads, saved, *groups)
    return result[0], result[1:]


def close_kernel(u_ref, saved_ref, w_ref, gain_ref, low_ref, middle_ref, second_ref):
    rows = u_ref.shape[0]
    lane = lane_of((rows, LANES))
    for j in range(H // 2):
        even = pltpu.roll(saved_ref[2 * j * rows : (2 * j + 1) * rows, :], HD, 1)
        odd = saved_ref[(2 * j + 1) * rows : (2 * j + 2) * rows, :]
        low_ref[:, j * LANES : (j + 1) * LANES] = jnp.where(lane < HD, even, odd).astype(BF16)
    last = pltpu.roll(saved_ref[(H - 1) * rows : H * rows, :], HD, 1)
    low_ref[:, (H - 1) * HD : H * HD] = last[:, :HD].astype(BF16)
    middle = u_ref[...].astype(F32) + dot_nn(low_ref[...], w_ref[...])
    middle_ref[...] = middle
    scale = lax.rsqrt(jnp.mean(middle * middle, axis=-1, keepdims=True) + EPSILON)
    second_ref[...] = (middle * scale * gain_ref[...].astype(F32)).astype(BF16)


def close_attention(u, saved, weight, gain):
    rows, width = u.shape
    return pl.pallas_call(
        close_kernel,
        out_shape=(
            jax.ShapeDtypeStruct((rows, QW), BF16),
            jax.ShapeDtypeStruct((rows, width), F32),
            jax.ShapeDtypeStruct((rows, width), BF16),
        ),
        in_specs=[WHOLE] * 4,
        out_specs=(WHOLE,) * 3,
        compiler_params=params(24),
        cost_estimate=cost(1.4),
        name="close_attention",
    )(u, saved, weight, gain)


def widen_kernel(*refs, count):
    pieces, w_ref, wide_ref, hidden_ref = refs[:count], *refs[count:]
    second = jnp.concatenate([piece[...] for piece in pieces], axis=0)
    wide = dot_nn(second, w_ref[...])
    wide_ref[...] = wide
    half = wide.shape[1] // 2
    gate, up = wide[:, :half], wide[:, half:]
    hidden_ref[...] = (gate * jax.nn.sigmoid(gate) * up).astype(BF16)


def widen(pieces, weight):
    count = len(pieces)
    rows, width = pieces[0].shape
    columns = weight.shape[1]
    return pl.pallas_call(
        functools.partial(widen_kernel, count=count),
        out_shape=(
            jax.ShapeDtypeStruct((count * rows, columns), F32),
            jax.ShapeDtypeStruct((count * rows, columns // 2), BF16),
        ),
        in_specs=[WHOLE] * (count + 1),
        out_specs=(WHOLE,) * 2,
        compiler_params=params(40),
        cost_estimate=cost(2.5),
        name="widen",
    )(*pieces, weight)


def narrow_kernel(hidden_ref, down_ref, later_ref, *outs):
    rows = outs[0].shape[0]
    for k, out in enumerate(outs):
        part = hidden_ref[k * rows : (k + 1) * rows, :]
        out[...] = dot_nt(part, down_ref[...]).astype(out.dtype)


def narrow(hidden, down, count, later):
    rows, width = hidden.shape[0] // count, down.shape[0]
    return pl.pallas_call(
        narrow_kernel,
        out_shape=(jax.ShapeDtypeStruct((rows, width), F32),)
        + tuple(jax.ShapeDtypeStruct((rows, width), BF16) for _ in range(count - 1)),
        in_specs=[WHOLE, WHOLE, pl.BlockSpec(memory_space=pl.ANY)],
        out_specs=(WHOLE,) * count,
        compiler_params=params(24),
        cost_estimate=cost(1.7),
        name="narrow",
    )(hidden, down, later)


def mlp_back_kernel(*refs, count):
    pieces, wide_ref, w_ref, down_ref = refs[:count], *refs[count : count + 3]
    grads_ref, outs = refs[count + 3], refs[count + 4 :]
    rows = pieces[0].shape[0]
    grad_y = jnp.concatenate([piece[...] for piece in pieces], axis=0)
    grad_hidden = dot_nn(grad_y, down_ref[...])
    half = wide_ref.shape[1] // 2
    gate, up = wide_ref[:, :half], wide_ref[:, half:]
    sig = jax.nn.sigmoid(gate)
    grads_ref[:, :half] = (grad_hidden * up * sig * (1.0 + gate * (1.0 - sig))).astype(BF16)
    grads_ref[:, half:] = (grad_hidden * gate * sig).astype(BF16)
    partial = dot_nt(grads_ref[...], w_ref[...])
    for k, out in enumerate(outs):
        out[...] = partial[k * rows : (k + 1) * rows].astype(out.dtype)


def mlp_back(pieces, wide, weight, down):
    count = len(pieces)
    rows, width = pieces[0].shape
    columns = weight.shape[1]
    result = pl.pallas_call(
        functools.partial(mlp_back_kernel, count=count),
        out_shape=(
            jax.ShapeDtypeStruct((count * rows, columns), BF16),
            jax.ShapeDtypeStruct((rows, width), F32),
        )
        + tuple(jax.ShapeDtypeStruct((rows, width), BF16) for _ in range(count - 1)),
        in_specs=[WHOLE] * (count + 3),
        out_specs=(WHOLE,) * (count + 1),
        compiler_params=params(40),
        cost_estimate=cost(4),
        name="mlp_back",
    )(*pieces, wide, weight, down)
    return result[0], result[1:]


def norm_back(values, gain, gradient):
    scaling = lax.rsqrt(jnp.mean(values * values, axis=-1, keepdims=True) + EPSILON)
    gain_grad = jnp.sum(gradient * values * scaling, axis=0, keepdims=True)
    scaled = gradient * gain.astype(F32)
    inner = jnp.mean(scaled * values, axis=-1, keepdims=True)
    return gain_grad, scaling * scaled - values * (scaling * scaling * scaling) * inner


def open_back_kernel(*refs, count):
    terms = refs[:count]
    middle_ref, gain_ref, y_ref, w_ref = refs[count : count + 4]
    grad_ref, low_ref, padded_ref, gain_grad_ref, wide_ref = refs[count + 4 :]
    gradient = terms[0][...]
    for term in terms[1:]:
        gradient = gradient + term[...].astype(F32)
    gain_grad, through = norm_back(middle_ref[...], gain_ref[...], gradient)
    gain_grad_ref[...] = gain_grad
    grad_middle = y_ref[...].astype(F32) + through
    grad_ref[...] = grad_middle
    low = grad_middle.astype(BF16)
    low_ref[...] = low
    wide_ref[:, :QW] = dot_nt(low, w_ref[...])
    lane = lane_of((low.shape[0], LANES))
    for h in range(H):
        block = wide_ref[:, h // 2 * LANES : (h // 2 + 1) * LANES]
        placed = block if h % 2 else pltpu.roll(block, HD, 1)
        padded_ref[:, h * LANES : (h + 1) * LANES] = jnp.where(lane < HD, 0.0, placed).astype(BF16)


def open_back(terms, middle, gain, grad_y, weight):
    rows, width = middle.shape
    count = len(terms)
    return pl.pallas_call(
        functools.partial(open_back_kernel, count=count),
        out_shape=(
            jax.ShapeDtypeStruct((rows, width), F32),
            jax.ShapeDtypeStruct((rows, width), BF16),
            jax.ShapeDtypeStruct((rows, H * LANES), BF16),
            jax.ShapeDtypeStruct((1, width), F32),
        ),
        in_specs=[WHOLE] * (count + 4),
        out_specs=(WHOLE,) * 4,
        scratch_shapes=[pltpu.VMEM((rows, (H + 1) // 2 * LANES), F32)],
        compiler_params=params(24),
        cost_estimate=cost(2),
        name="open_back",
    )(*terms, middle, gain, grad_y, weight)


def turned_back(block, cosine, sine, lane):
    return block * cosine - swap_halves(block, lane) * sine


def query_back_kernel(dq_ref, cos_ref, sin_ref, w_ref, mixed_ref, part_ref):
    cosine, sine = cos_ref[...], sin_ref[...]
    lane = lane_of(cosine.shape)

    def head(h):
        return turned_back(dq_ref[:, h * LANES : (h + 1) * LANES], cosine, sine, lane)

    for j in range(H // 2):
        block = jnp.where(lane < HD, head(2 * j), pltpu.roll(head(2 * j + 1), HD, 1))
        mixed_ref[:, j * LANES : (j + 1) * LANES] = block.astype(BF16)
    mixed_ref[:, (H - 1) * HD : QW] = head(H - 1)[:, :HD].astype(BF16)
    part_ref[...] = dot_nt(mixed_ref[...], w_ref[:, :QW])


def query_back(dq, cosine, sine, weight):
    rows, width = dq.shape[0], weight.shape[0]
    return pl.pallas_call(
        query_back_kernel,
        out_shape=(
            jax.ShapeDtypeStruct((rows, QW), BF16),
            jax.ShapeDtypeStruct((rows, width), F32),
        ),
        in_specs=[WHOLE] * 4,
        out_specs=(WHOLE,) * 2,
        compiler_params=params(24),
        cost_estimate=cost(1.2),
        name="query_back",
    )(dq, cosine, sine, weight)


def key_back_kernel(*refs, count):
    terms = refs[:count]
    part_ref, cos_ref, sin_ref, w_ref, u_ref, gain_ref, middle_ref = refs[count : count + 7]
    mixed_ref, out_ref, gain_grad_ref, wide_ref = refs[count + 7 :]
    grad_kv = terms[0][...].astype(F32)
    for term in terms[1:]:
        grad_kv = grad_kv + term[...].astype(F32)
    cosine, sine = cos_ref[...], sin_ref[...]
    lane = lane_of(cosine.shape)
    low = lane < HD
    blocks = [grad_kv[:, g * LANES : (g + 1) * LANES] for g in range(KVH)]
    keys = [turned_back(block, cosine, sine, lane) for block in blocks]

    def unit(h, high):
        block, at_high = (keys[h], False) if h < KVH else (blocks[h - KVH], True)
        return block if at_high == high else pltpu.roll(block, HD, 1)

    for j in range(KVH):
        block = jnp.where(low, unit(2 * j, False), unit(2 * j + 1, True))
        mixed_ref[:, j * LANES : (j + 1) * LANES] = block.astype(BF16)
    for j in range(KVH + 1):
        left = unit(2 * j - 1, False) if j else jnp.zeros(cosine.shape, F32)
        block = jnp.where(low, left, unit(2 * j, True)) if j < KVH else left
        wide_ref[:, j * LANES : (j + 1) * LANES] = block.astype(BF16)
    begin = QW // LANES * LANES
    columns = w_ref.shape[1] - begin
    gradient = part_ref[...] + dot_nt(wide_ref[:, :columns], w_ref[:, begin:])
    gain_grad, through = norm_back(u_ref[...].astype(F32), gain_ref[...], gradient)
    gain_grad_ref[...] = gain_grad
    out_ref[...] = (middle_ref[...] + through).astype(BF16)


def key_back(terms, part, cosine, sine, weight, u, gain, grad_middle):
    rows, width = u.shape
    count = len(terms)
    return pl.pallas_call(
        functools.partial(key_back_kernel, count=count),
        out_shape=(
            jax.ShapeDtypeStruct((rows, 2 * KW), BF16),
            jax.ShapeDtypeStruct((rows, width), BF16),
            jax.ShapeDtypeStruct((1, width), F32),
        ),
        in_specs=[WHOLE] * (count + 7),
        out_specs=(WHOLE,) * 3,
        scratch_shapes=[pltpu.VMEM((rows, 2 * KW + LANES), BF16)],
        compiler_params=params(24),
        cost_estimate=cost(2),
        name="key_back",
    )(*terms, part, cosine, sine, weight, u, gain, grad_middle)


def finish_kernel(index_ref, mine_ref, other_ref, gate_ref, up_ref):
    wa, first = index_ref[0], index_ref[1] == 0
    rows = gate_ref.shape[0]
    width = mine_ref.shape[1]
    for k in range(mine_ref.shape[0] // rows):
        columns = pl.ds(pl.multiple_of((wa ^ k) * width, LANES), width)
        piece = slice(k * rows, (k + 1) * rows)
        mine, other = mine_ref[piece, :].astype(F32), other_ref[piece, :].astype(F32)
        gate_ref[:, columns] = jnp.where(first, mine, other)
        up_ref[:, columns] = jnp.where(first, other, mine)


def finish(index, mine, other, rows):
    total, width = mine.shape
    result = jax.ShapeDtypeStruct((rows, total // rows * width), F32)
    return pl.pallas_call(
        finish_kernel,
        out_shape=(result, result),
        in_specs=[SCALARS, WHOLE, WHOLE],
        out_specs=(WHOLE, WHOLE),
        compiler_params=params(24),
        cost_estimate=cost(3.3),
        name="finish",
    )(index, mine, other)


def to_sibling(value):
    return lax.ppermute(value, "section", [(0, 1), (1, 0)])


def to_peer(value, k):
    count = lax.axis_size("wa")
    return lax.ppermute(value, "wa", [(i, i ^ k) for i in range(count)])


def gather_wa(value):
    return [value] + [to_peer(value, k) for k in range(1, lax.axis_size("wa"))]


def send_wa(pieces):
    return [pieces[0]] + [to_peer(piece, k) for k, piece in enumerate(pieces) if k]


def rotates(count):
    return count <= 4


def gather_ctx(value):
    count = lax.axis_size("ctx")
    if not rotates(count):
        return lax.all_gather(value, "ctx", axis=0, tiled=True)
    pieces = [value]
    for k in range(1, count):
        pieces.append(lax.ppermute(value, "ctx", [(i, (i + k) % count) for i in range(count)]))
    return join(pieces)


def scatter_ctx(value):
    count = lax.axis_size("ctx")
    rows = value.shape[0] // count
    if not rotates(count):
        blocks = value.reshape(count, rows, value.shape[1])
        return list(lax.all_to_all(blocks, "ctx", 0, 0, tiled=True))
    pieces = [value[:rows]]
    for k in range(1, count):
        piece = value[k * rows : (k + 1) * rows]
        pieces.append(lax.ppermute(piece, "ctx", [(i, (i - k) % count) for i in range(count)]))
    return pieces


def at(value, index, size, dim):
    return lax.dynamic_slice_in_dim(value, index * size, size, dim)


def tie(values, after):
    values, after = tuple(values), tuple(after)
    anywhere = pl.BlockSpec(memory_space=pl.ANY)
    return pl.pallas_call(
        lambda *refs: None,
        out_shape=tuple(jax.ShapeDtypeStruct(value.shape, value.dtype) for value in values),
        in_specs=[anywhere] * (len(values) + len(after)),
        out_specs=(anywhere,) * len(values),
        input_output_aliases={i: i for i in range(len(values))},
        cost_estimate=cost(0),
        name="tie",
    )(*values, *after)


def added(terms):
    total = terms[0].astype(F32)
    for term in terms[1:]:
        total = total + term.astype(F32)
    return total


def per_device(
    block_input, out_cotangent, block_table, attn_gain, w_qkv, w_out, mlp_gain, w_gate, w_up, w_down
):
    section = lax.axis_index("section")
    wa = lax.axis_index("wa")
    ctx = lax.axis_index("ctx")
    wa_count = lax.axis_size("wa")
    ctx_count = lax.axis_size("ctx")
    layers = lax.axis_size("section")
    first = section == 0
    peers = range(wa_count)
    index = jnp.stack([wa, section]).astype(jnp.int32)
    micro_count, tok_rows, width = block_input.shape
    half_rows = tok_rows // 2
    shard_rows = w_qkv.shape[1]
    ff_part = w_down.shape[1]
    w_qkv, w_out, w_gate, w_up, w_down = (a[0] for a in (w_qkv, w_out, w_gate, w_up, w_down))
    w_down = w_down.T

    in_block = jnp.arange(half_rows, dtype=jnp.int32)
    table = block_table.reshape(-1, 2)

    def positions_of(devices):
        return (table[devices][..., None] * half_rows + in_block).reshape(-1)

    own_pos = positions_of((ctx * wa_count + wa)[None])
    steps = jnp.arange(ctx_count)
    sources = (ctx - steps) % ctx_count if rotates(ctx_count) else steps
    key_pos = jnp.stack([positions_of(sources * wa_count + (wa ^ k)) for k in peers])
    key_pos_column = key_pos.T
    qpos_column, qpos_row = own_pos[:, None], own_pos[None, :]
    inverse = ROPE_BASE ** (-(jnp.arange(HD // 2, dtype=F32) * 2.0) / HD)
    angles = own_pos.astype(F32)[:, None] * inverse[None, :]
    cosine = jnp.tile(jnp.cos(angles), (1, 2 * LANES // HD))
    sines = jnp.sin(angles)
    sine = jnp.tile(jnp.concatenate([-sines, sines], axis=1), (1, LANES // HD))

    kept_rows = shard_rows // 2 + 8
    step = shard_rows - kept_rows
    own_gains = jnp.concatenate([attn_gain, mlp_gain], axis=0)
    gain_rows = jnp.pad(own_gains, ((0, 14), (0, w_qkv.shape[1] - shard_rows)))

    def halves(shard, extra=None):
        def part(half):
            rows = lax.dynamic_slice_in_dim(shard, half * step, kept_rows, 0)
            return rows if extra is None else jnp.concatenate([rows, extra], axis=0)

        keep, other = part(section), to_sibling(part(1 - section))
        return jnp.where(first, keep, other), jnp.where(first, other, keep)

    def fetch_rows(part, after=()):
        if after:
            (part,) = tie((part,), after)
        pieces = gather_wa(part)
        mine = join(pieces)
        other = to_sibling(mine)
        whole = assemble(index, mine, other, wa_count, True, kept_rows, shard_rows, step)
        return whole, mine, pieces[1:]

    def gains_of(mine):
        rows = mine.reshape(wa_count, -1, mine.shape[1])[:, kept_rows : kept_rows + 2, :shard_rows]
        return rows[wa ^ jnp.arange(wa_count)].transpose(1, 0, 2).reshape(2, 1, width)

    def fetch_columns(part, after):
        pieces = send_wa(tie([at(part, wa ^ k, ff_part, 1) for k in peers], after))
        mine = join(pieces)
        return assemble_pair(index, mine, to_sibling(mine), shard_rows), pieces[1:]

    qkv_parts = halves(w_qkv, gain_rows)
    qkv, mine, pieces = fetch_rows(qkv_parts[0])
    out_parts = halves(w_out)
    crossing = to_sibling(jnp.where(first, w_up, w_gate))
    wide_parts = (jnp.where(first, w_gate, crossing), jnp.where(first, crossing, w_up))
    down_other = to_sibling(w_down)
    downs = (jnp.where(first, w_down, down_other), jnp.where(first, down_other, w_down))
    gains = [gains_of(mine)]
    out, _, pieces = fetch_rows(out_parts[0], pieces)
    qkv_last, mine, pieces = fetch_rows(qkv_parts[1], pieces)
    gains.append(gains_of(mine))
    qkvs, outs, wides = [qkv, qkv_last], [out], []

    terms = [lax.dynamic_index_in_dim(block_input, section, 0, keepdims=False)]
    cotangent = lax.dynamic_index_in_dim(out_cotangent, section, 0, keepdims=False)
    records, inputs = [], []
    for layer in range(layers):
        u, normed, queries, kv = project(terms, gains[layer][0], qkvs[layer], cosine, sine)
        if layer:
            out, _, pieces = fetch_rows(out_parts[layer], terms[1:])
            outs.append(out)
            (grad_y,) = tie((cotangent,), pieces)
            grad_ys = gather_wa(grad_y)
            pieces = grad_ys[1:]
        (group,) = tie((gather_ctx(kv),), pieces)
        groups = gather_wa(group)
        weight, pieces = fetch_columns(wide_parts[layer], groups[1:])
        wides.append(weight)
        saved = attend(qpos_column, key_pos, queries, groups)
        low, middle, second = close_attention(u, saved, outs[layer], gains[layer][1])
        seconds = gather_wa(*tie((second,), pieces))
        wide, hidden = widen(seconds, wides[layer])
        if layer < layers - 1:
            partial = narrow(hidden, downs[layer], wa_count, index)
            terms = [middle] + send_wa(partial)
        inputs.append(u)
        records.append((u, normed, queries, groups, saved, low, middle, seconds, wide, hidden))

    def over_cores(value, size, dim):
        keep = at(value, section, size, dim)
        other = to_sibling(at(value, 1 - section, size, dim))
        return (keep.astype(F32) + other.astype(F32)).astype(BF16)

    def blocked(value):
        return value.reshape(wa_count, 2, shard_rows // 2, value.shape[1])

    def rows_over_wa(blocks, after):
        half = over_cores(blocks, 1, 1)[:, 0]
        pieces = send_wa(tie([at(half, wa ^ k, 1, 0)[0] for k in peers], after))
        return added(pieces).astype(BF16), pieces[1:]

    def over_ctx(values, after):
        return lax.psum(tie(values, after) if after else tuple(values), "ctx")

    input_grads, gain_grads = [None] * layers, []
    sums, pending = {}, ()
    done = ()
    for layer in reversed(range(layers)):
        u, normed, queries, groups, saved, low, middle, seconds, wide, hidden = records[layer]
        if layer < layers - 1:
            (grad_y,) = tie((grad_y,), square_pieces)
            grad_ys = gather_wa(grad_y)
        grad_wide, partial = mlp_back(grad_ys, wide, wides[layer], downs[layer])
        if layer < layers - 1:
            partial = tie(partial, (sums["wide", layer + 1],))
        terms = send_wa(partial)
        grad_middle, grad_low, grad_heads, gain_two_grad = open_back(
            terms, middle, gains[layer][1], grad_y, outs[layer]
        )

        wide_grad = dot_tn(jnp.concatenate(seconds, axis=0), grad_wide).astype(BF16)
        down_grad = dot_tn(jnp.concatenate(grad_ys, axis=0), hidden).astype(BF16)
        wide_half = over_cores(wide_grad, ff_part, 1)
        down_half = over_cores(down_grad, width // 2, 0)
        pieces = [at(wide_half, wa ^ k, shard_rows, 0) for k in peers]
        pieces = send_wa(tie(pieces, (grad_heads,)))
        wide_rows = join(pieces)
        wide_pieces = pieces[1:]
        if pending:
            key_half, key_pieces = rows_over_wa(pending[0], (grad_heads,))
            wide_pieces = wide_pieces + key_pieces

        dq, dkv = attend_back(qpos_row, key_pos_column, queries, grad_heads, saved, groups)
        dkv = send_wa(tie(dkv, wide_pieces))
        gathered = added(dkv).astype(BF16)
        if layer == layers - 1:
            done = over_ctx((wide_rows,), done)
            sums["wide", layer] = done[0]
        else:
            (gathered,) = tie((gathered,), (sums["square", layer + 1],))
            done = over_ctx((wide_rows, down_half, key_half), done)
            sums["wide", layer], sums["down", layer], sums["key", layer + 1] = done

        terms = scatter_ctx(gathered)
        grad_query, part = query_back(dq, cosine, sine, qkvs[layer])
        out_grad = dot_tn(low, grad_low).astype(BF16)
        query_grad = dot_tn(normed, grad_query).astype(BF16)
        square_grad = jnp.concatenate([blocked(out_grad), blocked(query_grad)], axis=2)
        square_half, square_pieces = rows_over_wa(square_grad, dkv[1:])
        if layer == layers - 1:
            done = over_ctx((down_half, square_half), done)
            sums["down", layer], sums["square", layer] = done
        else:
            done = over_ctx((square_half,), done)
            sums["square", layer] = done[0]

        grad_key, grad_u, gain_one_grad = key_back(
            terms, part, cosine, sine, qkvs[layer], u, gains[layer][0], grad_middle
        )
        key_grad = blocked(dot_tn(normed, grad_key).astype(BF16))
        pending = (key_grad,)
        gain_grads = [gain_one_grad, gain_two_grad] + gain_grads
        input_grads[layer] = grad_u
        grad_y = grad_u

    tails = jnp.concatenate(gain_grads, axis=0).reshape(-1, wa_count, 1, shard_rows)
    tails = jnp.broadcast_to(
        tails.transpose(1, 2, 0, 3).astype(BF16), (wa_count, 2, 2 * layers, shard_rows)
    )
    tails = jnp.pad(tails, ((0, 0), (0, 0), (0, 4), (0, 2 * KW - shard_rows)))
    packed, pieces = rows_over_wa(jnp.concatenate([key_grad, tails], axis=2), square_pieces)
    if rotates(ctx_count):
        key_half = added(jnp.split(gather_ctx(packed), ctx_count, axis=0))
    else:
        key_half = lax.psum(packed, "ctx").astype(F32)
    gain_sums = key_half[shard_rows // 2 : shard_rows // 2 + 2 * layers, :shard_rows]
    sums["key", 0] = key_half[: shard_rows // 2].astype(BF16)

    hidden, middle = records[-1][-1], records[-1][6]
    partial = narrow(hidden, downs[-1], wa_count, pieces[-1])
    last_result = added([middle] + send_wa(partial)).astype(BF16)

    def swapped(values):
        mine = jnp.where(first, values[0], values[1])
        return mine, to_sibling(jnp.where(first, values[1], values[0]))

    def by_layer(values):
        mine, other = swapped(values)
        return jnp.where(first, mine, other), jnp.where(first, other, mine)

    def both(values):
        return jnp.stack(by_layer(values))[None]

    def halves_of(name):
        return [sums[name, layer] for layer in range(layers)]

    down_halves, square_halves, key_halves = (
        by_layer(halves_of(name)) for name in ("down", "square", "key")
    )
    gate_sum, up_sum = finish(index, *swapped(halves_of("wide")), shard_rows)
    half = shard_rows // 2
    out_sum = jnp.concatenate([part[:half] for part in square_halves], axis=0)
    query_sum = jnp.concatenate([part[half:] for part in square_halves], axis=0)
    qkv_sum = jnp.concatenate([query_sum, jnp.concatenate(key_halves, axis=0)], axis=1)
    gain_own = lax.dynamic_index_in_dim(gain_sums.reshape(layers, 2, shard_rows), section, 0)
    return (
        both([inputs[1], last_result]),
        both(input_grads),
        gain_own[:, 0],
        qkv_sum.astype(F32)[None],
        out_sum.astype(F32)[None],
        gain_own[:, 1],
        gate_sum[None],
        up_sum[None],
        jnp.concatenate(down_halves, axis=0).astype(F32).T[None],
    )


def solution(mesh):
    return jax.shard_map(
        per_device,
        mesh=mesh,
        in_specs=(
            P(None, ("ctx", "wa"), None),
            P(None, ("ctx", "wa"), None),
            P(),
            P("section", "wa"),
            P("section", "wa", None),
            P("section", "wa", None),
            P("section", "wa"),
            P("section", "wa", None),
            P("section", "wa", None),
            P("section", "wa", None),
        ),
        out_specs=(
            P("section", None, ("ctx", "wa"), None),
            P("section", None, ("ctx", "wa"), None),
            P("section", "wa"),
            P("section", "wa", None),
            P("section", "wa", None),
            P("section", "wa"),
            P("section", "wa", None),
            P("section", "wa", None),
            P("section", "wa", None),
        ),
        check_vma=False,
    )
```

```python
import functools

import jax
import jax.numpy as jnp
from jax import lax
from jax.experimental import pallas as pl
from jax.experimental.pallas import tpu as pltpu
from jax.sharding import PartitionSpec as P

H = 15
KVH = 5
HD = 64
GROUP = H // KVH
QW = H * HD
KW = KVH * HD
LANES = 128
KEY_CHUNK = 512

EPSILON = 1e-05
ROPE_BASE = 100000.0
MASKED = -1e30
FLOPS_PER_US = 1.15e9
SCALE = HD**-0.5
F32 = jnp.float32
BF16 = jnp.bfloat16

WHOLE = pl.BlockSpec(memory_space=pltpu.VMEM)
SCALARS = pl.BlockSpec(memory_space=pltpu.SMEM)


def params(mib):
    return pltpu.CompilerParams(vmem_limit_bytes=mib * 1024 * 1024)


def cost(us):
    return pl.CostEstimate(flops=int(us * FLOPS_PER_US), bytes_accessed=0, transcendentals=0)


def dot_nn(a, b):
    return lax.dot_general(a, b, (((1,), (0,)), ((), ())), preferred_element_type=F32)


def dot_nt(a, b):
    return lax.dot_general(a, b, (((1,), (1,)), ((), ())), preferred_element_type=F32)


def dot_tn(a, b):
    return lax.dot_general(a, b, (((0,), (0,)), ((), ())), preferred_element_type=F32)


def lane_of(shape):
    return lax.broadcasted_iota(jnp.int32, shape, 1)


def swap_halves(block, lane):
    ahead = pltpu.roll(block, LANES - HD // 2, 1)
    behind = pltpu.roll(block, HD // 2, 1)
    return jnp.where(lane % HD < HD // 2, ahead, behind)


def join_kernel(*refs, count):
    pieces, out_ref = refs[:count], refs[-1]
    rows, width = pieces[0].shape
    for k, piece in enumerate(pieces):
        out_ref[k * rows : (k + 1) * rows, :width] = piece[...]
    if out_ref.shape[1] > width:
        out_ref[:, width:] = jnp.zeros((out_ref.shape[0], out_ref.shape[1] - width), out_ref.dtype)


def join(pieces, after=()):
    rows, width = pieces[0].shape
    padded = -(-width // LANES) * LANES
    return pl.pallas_call(
        functools.partial(join_kernel, count=len(pieces)),
        out_shape=jax.ShapeDtypeStruct((rows * len(pieces), padded), pieces[0].dtype),
        in_specs=[WHOLE] * len(pieces) + [pl.BlockSpec(memory_space=pl.ANY)] * len(after),
        out_specs=WHOLE,
        compiler_params=params(24),
        cost_estimate=cost(1),
        name="join",
    )(*pieces, *after)


def assemble_kernel(index_ref, mine_ref, other_ref, out_ref, *, relative, rows, shard_rows, step):
    wa, section = index_ref[0], index_ref[1]
    count = out_ref.shape[0] // shard_rows
    part = mine_ref.shape[0] // count
    width = out_ref.shape[1]
    for k in range(count):
        base = ((wa ^ k) if relative else k) * shard_rows
        start = pl.multiple_of(base + section * step, 16)
        out_ref[pl.ds(start, rows), :] = mine_ref[k * part : k * part + rows, :width]
        start = pl.multiple_of(base + (1 - section) * step, 16)
        out_ref[pl.ds(start, rows), :] = other_ref[k * part : k * part + rows, :width]


def assemble(index, mine, other, width, count, relative, rows, shard_rows, step):
    total = shard_rows * count
    return pl.pallas_call(
        functools.partial(
            assemble_kernel, relative=relative, rows=rows, shard_rows=shard_rows, step=step
        ),
        out_shape=jax.ShapeDtypeStruct((total, width), BF16),
        in_specs=[SCALARS, WHOLE, WHOLE],
        out_specs=WHOLE,
        compiler_params=params(24),
        cost_estimate=cost(2),
        name="assemble",
    )(index, mine, other)


def pair_kernel(index_ref, mine_ref, other_ref, out_ref, *, shard_rows):
    wa, section = index_ref[0], index_ref[1]
    width = mine_ref.shape[1]
    left = pl.multiple_of(section * width, LANES)
    right = pl.multiple_of((1 - section) * width, LANES)
    for k in range(out_ref.shape[0] // shard_rows):
        rows = pl.ds(pl.multiple_of((wa ^ k) * shard_rows, 16), shard_rows)
        piece = slice(k * shard_rows, (k + 1) * shard_rows)
        out_ref[rows, pl.ds(left, width)] = mine_ref[piece, :]
        out_ref[rows, pl.ds(right, width)] = other_ref[piece, :]


def assemble_pair(index, mine, other, shard_rows):
    total, width = mine.shape
    return pl.pallas_call(
        functools.partial(pair_kernel, shard_rows=shard_rows),
        out_shape=jax.ShapeDtypeStruct((total, 2 * width), BF16),
        in_specs=[SCALARS, WHOLE, WHOLE],
        out_specs=WHOLE,
        compiler_params=params(24),
        cost_estimate=cost(2.4),
        name="assemble_pair",
    )(index, mine, other)


def project_kernel(*refs, count):
    terms, refs = refs[:count], refs[count:]
    gain_ref, w_ref, cos_ref, sin_ref, u_ref, normed_ref, q_ref, kv_ref, mixed_ref = refs
    u = terms[0][...].astype(F32)
    for term in terms[1:]:
        u = u + term[...].astype(F32)
    u_ref[...] = u.astype(BF16)
    u = u_ref[...].astype(F32)
    scale = lax.rsqrt(jnp.mean(u * u, axis=-1, keepdims=True) + EPSILON)
    normed = (u * scale * gain_ref[...].astype(F32)).astype(BF16)
    normed_ref[...] = normed
    mixed_ref[:, : w_ref.shape[1]] = dot_nn(normed, w_ref[...])
    cosine, sine = cos_ref[...], sin_ref[...]
    lane = lane_of(cosine.shape)
    low = lane < HD
    roped = {}

    def unit(h, high):
        j = h // 2
        if j not in roped:
            block = mixed_ref[:, j * LANES : (j + 1) * LANES]
            if h < H + KVH:
                block = block * cosine + swap_halves(block, lane) * sine
            roped[j] = block
        return roped[j] if (h % 2 == 1) == high else pltpu.roll(roped[j], HD, 1)

    for h in range(H):
        padded = jnp.where(low, unit(h, False) * SCALE, 0.0)
        q_ref[:, h * LANES : (h + 1) * LANES] = padded.astype(BF16)
    for g in range(KVH):
        both = jnp.where(low, unit(H + g, False), unit(H + KVH + g, True))
        kv_ref[:, g * LANES : (g + 1) * LANES] = both.astype(BF16)


def project(terms, gain, weight, cosine, sine):
    rows, width = terms[0].shape
    count = len(terms)
    columns = weight.shape[1]
    padded = -(-columns // LANES) * LANES
    return pl.pallas_call(
        functools.partial(project_kernel, count=count),
        out_shape=(
            jax.ShapeDtypeStruct((rows, width), BF16),
            jax.ShapeDtypeStruct((rows, width), BF16),
            jax.ShapeDtypeStruct((rows, H * LANES), BF16),
            jax.ShapeDtypeStruct((rows, KVH * LANES), BF16),
        ),
        in_specs=[WHOLE] * (count + 4),
        out_specs=(WHOLE,) * 4,
        scratch_shapes=[pltpu.VMEM((rows, padded), F32)],
        compiler_params=params(24),
        cost_estimate=cost(2),
        name="project",
    )(*terms, gain, weight, cosine, sine)


def stack_heads(ref):
    return jnp.concatenate(
        [ref[:, i * LANES : (i + 1) * LANES] for i in range(GROUP)], axis=0
    )


def attend_kernel(qpos_ref, kpos_ref, q_ref, *refs):
    kv_refs, out_ref = refs[:-1], refs[-1]
    queries = stack_heads(q_ref)
    qpos = jnp.concatenate([qpos_ref[...]] * GROUP, axis=0)
    rows = queries.shape[0]
    top = jnp.full((rows, 1), MASKED, F32)
    total = jnp.zeros((rows, 1), F32)
    acc = jnp.zeros((rows, LANES), F32)
    for k, kv_ref in enumerate(kv_refs):
        for start in range(0, kv_ref.shape[0], KEY_CHUNK):
            size = min(KEY_CHUNK, kv_ref.shape[0] - start)
            kv = kv_ref[start : start + size, :]
            kpos = kpos_ref[k : k + 1, start : start + size]
            scores = jnp.where(kpos <= qpos, dot_nt(queries, kv), MASKED)
            new_top = jnp.maximum(top, jnp.max(scores, axis=-1, keepdims=True))
            fresh = jnp.exp(scores - new_top)
            decay = jnp.exp(top - new_top)
            total = total * decay + jnp.sum(fresh, axis=-1, keepdims=True)
            acc = acc * decay + dot_nn(fresh.astype(BF16), kv)
            top = new_top
    lse = top + jnp.log(total)
    out_ref[...] = jnp.where(lane_of(acc.shape) < HD, lse, acc / total)


def attend(qpos, kpos, queries, groups):
    rows = queries.shape[0]
    keys = groups[0].shape[0]
    pairs = H * rows * keys * len(groups)
    return pl.pallas_call(
        attend_kernel,
        out_shape=jax.ShapeDtypeStruct((H * rows, LANES), F32),
        grid=(KVH,),
        in_specs=[
            pl.BlockSpec((rows, 1), lambda g: (0, 0)),
            pl.BlockSpec(kpos.shape, lambda g: (0, 0)),
            pl.BlockSpec((rows, GROUP * LANES), lambda g: (0, g)),
        ]
        + [pl.BlockSpec((keys, LANES), lambda g: (0, g)) for _ in groups],
        out_specs=pl.BlockSpec((GROUP * rows, LANES), lambda g: (g, 0)),
        compiler_params=params(40),
        cost_estimate=cost(9.6),
        name="attend",
    )(qpos, kpos, queries, *groups)


def attend_back_kernel(qpos_ref, kpos_ref, q_ref, g_ref, o_ref, *refs, count):
    kv_refs, dq_ref, dkv_refs = refs[:count], refs[-count - 1], refs[-count:]
    queries = stack_heads(q_ref)
    grads = stack_heads(g_ref)
    saved = o_ref[...]
    lse = jnp.transpose(saved)[0:1, :]
    delta = jnp.sum(jnp.transpose(grads.astype(F32) * saved), axis=0, keepdims=True)
    qpos = jnp.concatenate([qpos_ref[...]] * GROUP, axis=1)
    rows = queries.shape[0]
    acc = jnp.zeros((rows, LANES), F32)
    for k, kv_ref in enumerate(kv_refs):
        for start in range(0, kv_ref.shape[0], KEY_CHUNK):
            size = min(KEY_CHUNK, kv_ref.shape[0] - start)
            kv = kv_ref[start : start + size, :]
            kpos = kpos_ref[start : start + size, k : k + 1]
            scores = jnp.where(kpos <= qpos, dot_nt(kv, queries), MASKED)
            probs = jnp.exp(scores - lse)
            grad_probs = dot_nt(kv, grads)
            grad_scores = (probs * (grad_probs - delta)).astype(BF16)
            acc = acc + dot_tn(grad_scores, kv)
            dkv = dot_nn(grad_scores, queries) + dot_nn(probs.astype(BF16), grads)
            dkv_refs[k][start : start + size, :] = dkv.astype(BF16)
    tok = q_ref.shape[0]
    for i in range(GROUP):
        dq_ref[:, i * LANES : (i + 1) * LANES] = acc[i * tok : (i + 1) * tok] * SCALE


def attend_back(qpos_row, kpos_column, queries, grads, saved, groups, after):
    rows = queries.shape[0]
    keys = groups[0].shape[0]
    pairs = H * rows * keys * len(groups)
    heads = pl.BlockSpec((rows, GROUP * LANES), lambda g: (0, g))
    kv_block = pl.BlockSpec((keys, LANES), lambda g: (0, g))
    result = pl.pallas_call(
        functools.partial(attend_back_kernel, count=len(groups)),
        out_shape=(jax.ShapeDtypeStruct((rows, H * LANES), F32),)
        + tuple(jax.ShapeDtypeStruct(group.shape, BF16) for group in groups),
        grid=(KVH,),
        in_specs=[
            pl.BlockSpec((1, rows), lambda g: (0, 0)),
            pl.BlockSpec(kpos_column.shape, lambda g: (0, 0)),
            heads,
            heads,
            pl.BlockSpec((GROUP * rows, LANES), lambda g: (g, 0)),
        ]
        + [kv_block for _ in groups]
        + [pl.BlockSpec(memory_space=pl.ANY) for _ in after],
        out_specs=(heads,) + tuple(kv_block for _ in groups),
        compiler_params=params(40),
        cost_estimate=cost(15.2),
        name="attend_back",
    )(qpos_row, kpos_column, queries, grads, saved, *groups, *after)
    return result[0], result[1:]


def close_kernel(u_ref, saved_ref, w_ref, gain_ref, low_ref, middle_ref, second_ref):
    rows = u_ref.shape[0]
    lane = lane_of((rows, LANES))
    for j in range(H // 2):
        even = pltpu.roll(saved_ref[2 * j * rows : (2 * j + 1) * rows, :], HD, 1)
        odd = saved_ref[(2 * j + 1) * rows : (2 * j + 2) * rows, :]
        low_ref[:, j * LANES : (j + 1) * LANES] = jnp.where(lane < HD, even, odd).astype(BF16)
    last = pltpu.roll(saved_ref[(H - 1) * rows : H * rows, :], HD, 1)
    low_ref[:, (H - 1) * HD : H * HD] = last[:, :HD].astype(BF16)
    middle = u_ref[...].astype(F32) + dot_nn(low_ref[...], w_ref[...])
    middle_ref[...] = middle
    scale = lax.rsqrt(jnp.mean(middle * middle, axis=-1, keepdims=True) + EPSILON)
    second_ref[...] = (middle * scale * gain_ref[...].astype(F32)).astype(BF16)


def close_attention(u, saved, weight, gain):
    rows, width = u.shape
    return pl.pallas_call(
        close_kernel,
        out_shape=(
            jax.ShapeDtypeStruct((rows, QW), BF16),
            jax.ShapeDtypeStruct((rows, width), F32),
            jax.ShapeDtypeStruct((rows, width), BF16),
        ),
        in_specs=[WHOLE] * 4,
        out_specs=(WHOLE,) * 3,
        compiler_params=params(24),
        cost_estimate=cost(1.4),
        name="close_attention",
    )(u, saved, weight, gain)


def widen_kernel(*refs, count):
    pieces, w_ref, wide_ref, hidden_ref = refs[:count], *refs[count:]
    second = jnp.concatenate([piece[...] for piece in pieces], axis=0)
    wide = dot_nn(second, w_ref[...])
    wide_ref[...] = wide
    half = wide.shape[1] // 2
    gate, up = wide[:, :half], wide[:, half:]
    hidden_ref[...] = (gate * jax.nn.sigmoid(gate) * up).astype(BF16)


def widen(pieces, weight):
    count = len(pieces)
    rows, width = pieces[0].shape
    columns = weight.shape[1]
    return pl.pallas_call(
        functools.partial(widen_kernel, count=count),
        out_shape=(
            jax.ShapeDtypeStruct((count * rows, columns), F32),
            jax.ShapeDtypeStruct((count * rows, columns // 2), BF16),
        ),
        in_specs=[WHOLE] * (count + 1),
        out_specs=(WHOLE,) * 2,
        compiler_params=params(40),
        cost_estimate=cost(2.5),
        name="widen",
    )(*pieces, weight)


def narrow_kernel(hidden_ref, down_ref, later_ref, *outs):
    rows = outs[0].shape[0]
    for k, out in enumerate(outs):
        part = hidden_ref[k * rows : (k + 1) * rows, :]
        out[...] = dot_nt(part, down_ref[...]).astype(out.dtype)


def narrow(hidden, down, count, later):
    rows, width = hidden.shape[0] // count, down.shape[0]
    return pl.pallas_call(
        narrow_kernel,
        out_shape=(jax.ShapeDtypeStruct((rows, width), F32),)
        + tuple(jax.ShapeDtypeStruct((rows, width), BF16) for _ in range(count - 1)),
        in_specs=[WHOLE, WHOLE, pl.BlockSpec(memory_space=pl.ANY)],
        out_specs=(WHOLE,) * count,
        compiler_params=params(24),
        cost_estimate=cost(1.7),
        name="narrow",
    )(hidden, down, later)


def mlp_back_kernel(*refs, count):
    pieces, wide_ref, w_ref, down_ref = refs[:count], *refs[count : count + 3]
    grads_ref, outs = refs[count + 3], refs[count + 4 :]
    rows = pieces[0].shape[0]
    grad_y = jnp.concatenate([piece[...] for piece in pieces], axis=0)
    grad_hidden = dot_nn(grad_y, down_ref[...])
    half = wide_ref.shape[1] // 2
    gate, up = wide_ref[:, :half], wide_ref[:, half:]
    sig = jax.nn.sigmoid(gate)
    grads_ref[:, :half] = (grad_hidden * up * sig * (1.0 + gate * (1.0 - sig))).astype(BF16)
    grads_ref[:, half:] = (grad_hidden * gate * sig).astype(BF16)
    partial = dot_nt(grads_ref[...], w_ref[...])
    for k, out in enumerate(outs):
        out[...] = partial[k * rows : (k + 1) * rows].astype(out.dtype)


def mlp_back(pieces, wide, weight, down):
    count = len(pieces)
    rows, width = pieces[0].shape
    columns = weight.shape[1]
    result = pl.pallas_call(
        functools.partial(mlp_back_kernel, count=count),
        out_shape=(
            jax.ShapeDtypeStruct((count * rows, columns), BF16),
            jax.ShapeDtypeStruct((rows, width), F32),
        )
        + tuple(jax.ShapeDtypeStruct((rows, width), BF16) for _ in range(count - 1)),
        in_specs=[WHOLE] * (count + 3),
        out_specs=(WHOLE,) * (count + 1),
        compiler_params=params(40),
        cost_estimate=cost(4),
        name="mlp_back",
    )(*pieces, wide, weight, down)
    return result[0], result[1:]


def norm_back(values, gain, gradient):
    scaling = lax.rsqrt(jnp.mean(values * values, axis=-1, keepdims=True) + EPSILON)
    gain_grad = jnp.sum(gradient * values * scaling, axis=0, keepdims=True)
    scaled = gradient * gain.astype(F32)
    inner = jnp.mean(scaled * values, axis=-1, keepdims=True)
    return gain_grad, scaling * scaled - values * (scaling * scaling * scaling) * inner


def open_back_kernel(*refs, count):
    terms = refs[:count]
    middle_ref, gain_ref, y_ref, w_ref = refs[count : count + 4]
    grad_ref, low_ref, padded_ref, gain_grad_ref, wide_ref = refs[count + 4 :]
    gradient = terms[0][...]
    for term in terms[1:]:
        gradient = gradient + term[...].astype(F32)
    gain_grad, through = norm_back(middle_ref[...], gain_ref[...], gradient)
    gain_grad_ref[...] = gain_grad
    grad_middle = y_ref[...].astype(F32) + through
    grad_ref[...] = grad_middle
    low = grad_middle.astype(BF16)
    low_ref[...] = low
    wide_ref[:, :QW] = dot_nt(low, w_ref[...])
    lane = lane_of((low.shape[0], LANES))
    for h in range(H):
        block = wide_ref[:, h // 2 * LANES : (h // 2 + 1) * LANES]
        placed = block if h % 2 else pltpu.roll(block, HD, 1)
        padded_ref[:, h * LANES : (h + 1) * LANES] = jnp.where(lane < HD, 0.0, placed).astype(BF16)


def open_back(terms, middle, gain, grad_y, weight):
    rows, width = middle.shape
    count = len(terms)
    return pl.pallas_call(
        functools.partial(open_back_kernel, count=count),
        out_shape=(
            jax.ShapeDtypeStruct((rows, width), F32),
            jax.ShapeDtypeStruct((rows, width), BF16),
            jax.ShapeDtypeStruct((rows, H * LANES), BF16),
            jax.ShapeDtypeStruct((1, width), F32),
        ),
        in_specs=[WHOLE] * (count + 4),
        out_specs=(WHOLE,) * 4,
        scratch_shapes=[pltpu.VMEM((rows, (H + 1) // 2 * LANES), F32)],
        compiler_params=params(24),
        cost_estimate=cost(2),
        name="open_back",
    )(*terms, middle, gain, grad_y, weight)


def turned_back(block, cosine, sine, lane):
    return block * cosine - swap_halves(block, lane) * sine


def query_back_kernel(dq_ref, cos_ref, sin_ref, w_ref, mixed_ref, part_ref):
    cosine, sine = cos_ref[...], sin_ref[...]
    lane = lane_of(cosine.shape)

    def head(h):
        return turned_back(dq_ref[:, h * LANES : (h + 1) * LANES], cosine, sine, lane)

    for j in range(H // 2):
        block = jnp.where(lane < HD, head(2 * j), pltpu.roll(head(2 * j + 1), HD, 1))
        mixed_ref[:, j * LANES : (j + 1) * LANES] = block.astype(BF16)
    mixed_ref[:, (H - 1) * HD : QW] = head(H - 1)[:, :HD].astype(BF16)
    part_ref[...] = dot_nt(mixed_ref[...], w_ref[:, :QW])


def query_back(dq, cosine, sine, weight):
    rows, width = dq.shape[0], weight.shape[0]
    return pl.pallas_call(
        query_back_kernel,
        out_shape=(
            jax.ShapeDtypeStruct((rows, QW), BF16),
            jax.ShapeDtypeStruct((rows, width), F32),
        ),
        in_specs=[WHOLE] * 4,
        out_specs=(WHOLE,) * 2,
        compiler_params=params(24),
        cost_estimate=cost(1.2),
        name="query_back",
    )(dq, cosine, sine, weight)


def key_back_kernel(*refs, count):
    terms = refs[:count]
    part_ref, cos_ref, sin_ref, w_ref, u_ref, gain_ref, middle_ref = refs[count : count + 7]
    mixed_ref, out_ref, gain_grad_ref, wide_ref = refs[count + 7 :]
    grad_kv = terms[0][...].astype(F32)
    for term in terms[1:]:
        grad_kv = grad_kv + term[...].astype(F32)
    cosine, sine = cos_ref[...], sin_ref[...]
    lane = lane_of(cosine.shape)
    low = lane < HD
    blocks = [grad_kv[:, g * LANES : (g + 1) * LANES] for g in range(KVH)]
    keys = [turned_back(block, cosine, sine, lane) for block in blocks]

    def unit(h, high):
        block, at_high = (keys[h], False) if h < KVH else (blocks[h - KVH], True)
        return block if at_high == high else pltpu.roll(block, HD, 1)

    for j in range(KVH):
        block = jnp.where(low, unit(2 * j, False), unit(2 * j + 1, True))
        mixed_ref[:, j * LANES : (j + 1) * LANES] = block.astype(BF16)
    for j in range(KVH + 1):
        left = unit(2 * j - 1, False) if j else jnp.zeros(cosine.shape, F32)
        block = jnp.where(low, left, unit(2 * j, True)) if j < KVH else left
        wide_ref[:, j * LANES : (j + 1) * LANES] = block.astype(BF16)
    begin = QW // LANES * LANES
    columns = w_ref.shape[1] - begin
    gradient = part_ref[...] + dot_nt(wide_ref[:, :columns], w_ref[:, begin:])
    gain_grad, through = norm_back(u_ref[...].astype(F32), gain_ref[...], gradient)
    gain_grad_ref[...] = gain_grad
    out_ref[...] = (middle_ref[...] + through).astype(BF16)


def key_back(terms, part, cosine, sine, weight, u, gain, grad_middle):
    rows, width = u.shape
    count = len(terms)
    return pl.pallas_call(
        functools.partial(key_back_kernel, count=count),
        out_shape=(
            jax.ShapeDtypeStruct((rows, 2 * KW), BF16),
            jax.ShapeDtypeStruct((rows, width), BF16),
            jax.ShapeDtypeStruct((1, width), F32),
        ),
        in_specs=[WHOLE] * (count + 7),
        out_specs=(WHOLE,) * 3,
        scratch_shapes=[pltpu.VMEM((rows, 2 * KW + LANES), BF16)],
        compiler_params=params(24),
        cost_estimate=cost(2),
        name="key_back",
    )(*terms, part, cosine, sine, weight, u, gain, grad_middle)


def finish_kernel(index_ref, mine_ref, other_ref, gate_ref, up_ref):
    wa, first = index_ref[0], index_ref[1] == 0
    rows = gate_ref.shape[0]
    width = mine_ref.shape[1]
    for k in range(mine_ref.shape[0] // rows):
        columns = pl.ds(pl.multiple_of((wa ^ k) * width, LANES), width)
        piece = slice(k * rows, (k + 1) * rows)
        mine, other = mine_ref[piece, :].astype(F32), other_ref[piece, :].astype(F32)
        gate_ref[:, columns] = jnp.where(first, mine, other)
        up_ref[:, columns] = jnp.where(first, other, mine)


def finish(index, mine, other, rows):
    total, width = mine.shape
    result = jax.ShapeDtypeStruct((rows, total // rows * width), F32)
    return pl.pallas_call(
        finish_kernel,
        out_shape=(result, result),
        in_specs=[SCALARS, WHOLE, WHOLE],
        out_specs=(WHOLE, WHOLE),
        compiler_params=params(24),
        cost_estimate=cost(3.3),
        name="finish",
    )(index, mine, other)


def to_sibling(value):
    return lax.ppermute(value, "section", [(0, 1), (1, 0)])


def to_peer(value, k):
    count = lax.axis_size("wa")
    return lax.ppermute(value, "wa", [(i, i ^ k) for i in range(count)])


def gather_wa(value):
    return [value] + [to_peer(value, k) for k in range(1, lax.axis_size("wa"))]


def send_wa(pieces):
    return [pieces[0]] + [to_peer(piece, k) for k, piece in enumerate(pieces) if k]


def rotates(count):
    return count <= 4


def gather_ctx(value):
    count = lax.axis_size("ctx")
    if not rotates(count):
        return lax.all_gather(value, "ctx", axis=0, tiled=True)
    pieces = [value]
    for k in range(1, count):
        pieces.append(lax.ppermute(value, "ctx", [(i, (i + k) % count) for i in range(count)]))
    return join(pieces)


def scatter_ctx(value):
    count = lax.axis_size("ctx")
    rows = value.shape[0] // count
    if not rotates(count):
        blocks = value.reshape(count, rows, value.shape[1])
        return list(lax.all_to_all(blocks, "ctx", 0, 0, tiled=True))
    pieces = [value[:rows]]
    for k in range(1, count):
        piece = value[k * rows : (k + 1) * rows]
        pieces.append(lax.ppermute(piece, "ctx", [(i, (i - k) % count) for i in range(count)]))
    return pieces


def at(value, index, size, dim):
    return lax.dynamic_slice_in_dim(value, index * size, size, dim)


def tie(values, after):
    values, after = tuple(values), tuple(after)
    anywhere = pl.BlockSpec(memory_space=pl.ANY)
    return pl.pallas_call(
        lambda *refs: None,
        out_shape=tuple(jax.ShapeDtypeStruct(value.shape, value.dtype) for value in values),
        in_specs=[anywhere] * (len(values) + len(after)),
        out_specs=(anywhere,) * len(values),
        input_output_aliases={i: i for i in range(len(values))},
        cost_estimate=cost(0),
        name="tie",
    )(*values, *after)


def added(terms):
    total = terms[0].astype(F32)
    for term in terms[1:]:
        total = total + term.astype(F32)
    return total


def per_device(
    block_input, out_cotangent, block_table, attn_gain, w_qkv, w_out, mlp_gain, w_gate, w_up, w_down
):
    section = lax.axis_index("section")
    wa = lax.axis_index("wa")
    ctx = lax.axis_index("ctx")
    wa_count = lax.axis_size("wa")
    ctx_count = lax.axis_size("ctx")
    layers = lax.axis_size("section")
    first = section == 0
    peers = range(wa_count)
    index = jnp.stack([wa, section]).astype(jnp.int32)
    micro_count, tok_rows, width = block_input.shape
    half_rows = tok_rows // 2
    shard_rows = w_qkv.shape[1]
    ff_part = w_down.shape[1]
    w_qkv, w_out, w_gate, w_up, w_down = (a[0] for a in (w_qkv, w_out, w_gate, w_up, w_down))
    w_down = w_down.T

    in_block = jnp.arange(half_rows, dtype=jnp.int32)
    table = block_table.reshape(-1, 2)

    def positions_of(devices):
        return (table[devices][..., None] * half_rows + in_block).reshape(-1)

    own_pos = positions_of((ctx * wa_count + wa)[None])
    steps = jnp.arange(ctx_count)
    sources = (ctx - steps) % ctx_count if rotates(ctx_count) else steps
    key_pos = jnp.stack([positions_of(sources * wa_count + (wa ^ k)) for k in peers])
    key_pos_column = key_pos.T
    qpos_column, qpos_row = own_pos[:, None], own_pos[None, :]
    inverse = ROPE_BASE ** (-(jnp.arange(HD // 2, dtype=F32) * 2.0) / HD)
    angles = own_pos.astype(F32)[:, None] * inverse[None, :]
    cosine = jnp.tile(jnp.cos(angles), (1, 2 * LANES // HD))
    sines = jnp.sin(angles)
    sine = jnp.tile(jnp.concatenate([-sines, sines], axis=1), (1, LANES // HD))

    kept_rows = shard_rows // 2 + 8
    step = shard_rows - kept_rows
    own_gains = jnp.concatenate([attn_gain, mlp_gain], axis=0)
    gain_rows = jnp.pad(own_gains, ((0, 14), (0, w_qkv.shape[1] - shard_rows)))

    def halves(shard, extra=None):
        def part(half):
            rows = lax.dynamic_slice_in_dim(shard, half * step, kept_rows, 0)
            return rows if extra is None else jnp.concatenate([rows, extra], axis=0)

        keep, other = part(section), to_sibling(part(1 - section))
        return jnp.where(first, keep, other), jnp.where(first, other, keep)

    def fetch_rows(part, after=()):
        if after:
            (part,) = tie((part,), after)
        return gather_wa(part)

    def placed_rows(pieces, after=()):
        mine = join(pieces, after)
        columns = pieces[0].shape[1]
        return assemble(
            index, mine, to_sibling(mine), columns, wa_count, True, kept_rows, shard_rows, step
        )

    def gains_of(pieces):
        rows = jnp.stack([piece[kept_rows : kept_rows + 2, :shard_rows] for piece in pieces])
        return rows[wa ^ jnp.arange(wa_count)].transpose(1, 0, 2).reshape(2, 1, width)

    def fetch_columns(part, after):
        return send_wa(tie([at(part, wa ^ k, ff_part, 1) for k in peers], after))

    def placed_columns(pieces, after):
        mine = join(pieces, after)
        return assemble_pair(index, mine, to_sibling(mine), shard_rows)

    qkv_parts = halves(w_qkv, gain_rows)
    qkv_pieces = fetch_rows(qkv_parts[0])
    qkv = placed_rows(qkv_pieces)
    out_parts = halves(w_out)
    crossing = to_sibling(jnp.where(first, w_up, w_gate))
    wide_parts = (jnp.where(first, w_gate, crossing), jnp.where(first, crossing, w_up))
    down_other = to_sibling(w_down)
    downs = (jnp.where(first, w_down, down_other), jnp.where(first, down_other, w_down))
    out_pieces = fetch_rows(out_parts[0], qkv_pieces[1:])
    last_pieces = fetch_rows(qkv_parts[1], out_pieces[1:])
    gains = [gains_of(qkv_pieces), gains_of(last_pieces)]
    qkvs, outs, wides = [qkv], [], []

    terms = [lax.dynamic_index_in_dim(block_input, section, 0, keepdims=False)]
    cotangent = lax.dynamic_index_in_dim(out_cotangent, section, 0, keepdims=False)
    records, inputs = [], []
    for layer in range(layers):
        u, normed, queries, kv = project(terms, gains[layer][0], qkvs[layer], cosine, sine)
        pieces = last_pieces[1:]
        if layer:
            out_pieces = fetch_rows(out_parts[layer], terms[1:])
            (grad_y,) = tie((cotangent,), out_pieces[1:])
            grad_ys = gather_wa(grad_y)
            pieces = grad_ys[1:]
        group = gather_ctx(kv)
        outs.append(placed_rows(out_pieces, (group,)))
        (group,) = tie((group,), pieces)
        groups = gather_wa(group)
        wide_pieces = fetch_columns(wide_parts[layer], groups[1:])
        saved = attend(qpos_column, key_pos, queries, groups)
        wides.append(placed_columns(wide_pieces, (saved,)))
        if not layer:
            qkvs.append(placed_rows(last_pieces, (saved,)))
        low, middle, second = close_attention(u, saved, outs[layer], gains[layer][1])
        seconds = gather_wa(*tie((second,), wide_pieces[1:]))
        wide, hidden = widen(seconds, wides[layer])
        if layer < layers - 1:
            partial = narrow(hidden, downs[layer], wa_count, index)
            terms = [middle] + send_wa(partial)
        inputs.append(u)
        records.append((u, normed, queries, groups, saved, low, middle, seconds, wide, hidden))

    def over_cores(value, size, dim):
        keep = at(value, section, size, dim)
        other = to_sibling(at(value, 1 - section, size, dim))
        return (keep.astype(F32) + other.astype(F32)).astype(BF16)

    def blocked(value):
        return value.reshape(wa_count, 2, shard_rows // 2, value.shape[1])

    def rows_over_wa(blocks, after):
        half = over_cores(blocks, 1, 1)[:, 0]
        pieces = [at(half, wa ^ k, 1, 0)[0] for k in peers]
        pieces = send_wa(tie(pieces, after) if after else pieces)
        return added(pieces).astype(BF16), pieces[1:]

    def over_ctx(values, turn):
        order = [(i + turn) % ctx_count for i in range(ctx_count)]
        return lax.psum(tuple(values), "ctx", axis_index_groups=[order])

    input_grads, gain_grads = [None] * layers, []
    sums, pending = {}, ()
    for layer in reversed(range(layers)):
        u, normed, queries, groups, saved, low, middle, seconds, wide, hidden = records[layer]
        if layer < layers - 1:
            grad_ys = gather_wa(grad_y)
        grad_wide, partial = mlp_back(grad_ys, wide, wides[layer], downs[layer])
        terms = send_wa(partial)
        grad_middle, grad_low, grad_heads, gain_two_grad = open_back(
            terms, middle, gains[layer][1], grad_y, outs[layer]
        )

        wide_grad = dot_tn(jnp.concatenate(seconds, axis=0), grad_wide).astype(BF16)
        down_grad = dot_tn(jnp.concatenate(grad_ys, axis=0), hidden).astype(BF16)
        wide_half = over_cores(wide_grad, ff_part, 1)
        down_half = over_cores(down_grad, width // 2, 0)
        pieces = [at(wide_half, wa ^ k, shard_rows, 0) for k in peers]
        pieces = send_wa(pieces)
        wide_rows = join(pieces)
        wide_pieces = pieces[1:]
        before = (wide_rows, down_half)
        if pending:
            key_half, _ = rows_over_wa(pending[0], ())
            before = (wide_rows, key_half)

        dq, dkv = attend_back(
            qpos_row, key_pos_column, queries, grad_heads, saved, groups, before
        )
        if layer < layers - 1:
            dkv = tie(dkv, done)
        dkv = send_wa(dkv)
        gathered = added(dkv).astype(BF16)
        if layer == layers - 1:
            done = over_ctx((wide_rows, down_half), 0)
            sums["wide", layer], sums["down", layer] = done
        else:
            done = over_ctx((key_half, wide_rows, down_half), 1)
            sums["key", layer + 1], sums["wide", layer], sums["down", layer] = done
            last_square = square_half

        terms = scatter_ctx(gathered)
        grad_query, part = query_back(dq, cosine, sine, qkvs[layer])
        out_grad = dot_tn(low, grad_low).astype(BF16)
        query_grad = dot_tn(normed, grad_query).astype(BF16)
        square_grad = jnp.concatenate([blocked(out_grad), blocked(query_grad)], axis=2)
        square_half, square_pieces = rows_over_wa(square_grad, ())
        if layer == 0:
            done = over_ctx(tie((last_square, square_half), done), 2)
            sums["square", layer + 1], sums["square", layer] = done

        grad_key, grad_u, gain_one_grad = key_back(
            terms, part, cosine, sine, qkvs[layer], u, gains[layer][0], grad_middle
        )
        key_grad = blocked(dot_tn(normed, grad_key).astype(BF16))
        pending = (key_grad,)
        gain_grads = [gain_one_grad, gain_two_grad] + gain_grads
        input_grads[layer] = grad_u
        grad_y = grad_u

    tails = jnp.concatenate(gain_grads, axis=0).reshape(-1, wa_count, 1, shard_rows)
    tails = jnp.broadcast_to(
        tails.transpose(1, 2, 0, 3).astype(BF16), (wa_count, 2, 2 * layers, shard_rows)
    )
    tails = jnp.pad(tails, ((0, 0), (0, 0), (0, 4), (0, 2 * KW - shard_rows)))
    packed, pieces = rows_over_wa(jnp.concatenate([key_grad, tails], axis=2), square_pieces)
    if rotates(ctx_count):
        key_half = added(jnp.split(gather_ctx(packed), ctx_count, axis=0))
    else:
        key_half = lax.psum(packed, "ctx").astype(F32)
    gain_sums = key_half[shard_rows // 2 : shard_rows // 2 + 2 * layers, :shard_rows]
    sums["key", 0] = key_half[: shard_rows // 2].astype(BF16)

    hidden, middle = records[-1][-1], records[-1][6]
    partial = narrow(hidden, downs[-1], wa_count, pieces[-1])
    last_result = added([middle] + send_wa(partial)).astype(BF16)

    def swapped(values):
        mine = jnp.where(first, values[0], values[1])
        return mine, to_sibling(jnp.where(first, values[1], values[0]))

    def by_layer(values):
        mine, other = swapped(values)
        return jnp.where(first, mine, other), jnp.where(first, other, mine)

    def both(values):
        return jnp.stack(by_layer(values))[None]

    def halves_of(name):
        return [sums[name, layer] for layer in range(layers)]

    down_halves, square_halves, key_halves = (
        by_layer(halves_of(name)) for name in ("down", "square", "key")
    )
    gate_sum, up_sum = finish(index, *swapped(halves_of("wide")), shard_rows)
    half = shard_rows // 2
    out_sum = jnp.concatenate([part[:half] for part in square_halves], axis=0)
    query_sum = jnp.concatenate([part[half:] for part in square_halves], axis=0)
    qkv_sum = jnp.concatenate([query_sum, jnp.concatenate(key_halves, axis=0)], axis=1)
    gain_own = lax.dynamic_index_in_dim(gain_sums.reshape(layers, 2, shard_rows), section, 0)
    return (
        both([inputs[1], last_result]),
        both(input_grads),
        gain_own[:, 0],
        qkv_sum.astype(F32)[None],
        out_sum.astype(F32)[None],
        gain_own[:, 1],
        gate_sum[None],
        up_sum[None],
        jnp.concatenate(down_halves, axis=0).astype(F32).T[None],
    )


def solution(mesh):
    return jax.shard_map(
        per_device,
        mesh=mesh,
        in_specs=(
            P(None, ("ctx", "wa"), None),
            P(None, ("ctx", "wa"), None),
            P(),
            P("section", "wa"),
            P("section", "wa", None),
            P("section", "wa", None),
            P("section", "wa"),
            P("section", "wa", None),
            P("section", "wa", None),
            P("section", "wa", None),
        ),
        out_specs=(
            P("section", None, ("ctx", "wa"), None),
            P("section", None, ("ctx", "wa"), None),
            P("section", "wa"),
            P("section", "wa", None),
            P("section", "wa", None),
            P("section", "wa"),
            P("section", "wa", None),
            P("section", "wa", None),
            P("section", "wa", None),
        ),
        check_vma=False,
    )
```

```python
import functools

import jax
import jax.numpy as jnp
from jax import lax
from jax.experimental import pallas as pl
from jax.experimental.pallas import tpu as pltpu
from jax.sharding import PartitionSpec as P

H = 15
KVH = 5
HD = 64
GROUP = H // KVH
QW = H * HD
KW = KVH * HD
LANES = 128
KEY_CHUNK = 512

EPSILON = 1e-05
ROPE_BASE = 100000.0
MASKED = -1e30
FLOPS_PER_US = 1.15e9
SCALE = HD**-0.5
F32 = jnp.float32
BF16 = jnp.bfloat16

WHOLE = pl.BlockSpec(memory_space=pltpu.VMEM)
SCALARS = pl.BlockSpec(memory_space=pltpu.SMEM)


def params(mib):
    return pltpu.CompilerParams(vmem_limit_bytes=mib * 1024 * 1024)


def cost(us):
    return pl.CostEstimate(flops=int(us * FLOPS_PER_US), bytes_accessed=0, transcendentals=0)


def dot_nn(a, b):
    return lax.dot_general(a, b, (((1,), (0,)), ((), ())), preferred_element_type=F32)


def dot_nt(a, b):
    return lax.dot_general(a, b, (((1,), (1,)), ((), ())), preferred_element_type=F32)


def dot_tn(a, b):
    return lax.dot_general(a, b, (((0,), (0,)), ((), ())), preferred_element_type=F32)


def lane_of(shape):
    return lax.broadcasted_iota(jnp.int32, shape, 1)


def swap_halves(block, lane):
    ahead = pltpu.roll(block, LANES - HD // 2, 1)
    behind = pltpu.roll(block, HD // 2, 1)
    return jnp.where(lane % HD < HD // 2, ahead, behind)


def join_kernel(*refs, count):
    pieces, out_ref = refs[:count], refs[-1]
    rows, width = pieces[0].shape
    for k, piece in enumerate(pieces):
        out_ref[k * rows : (k + 1) * rows, :width] = piece[...]
    if out_ref.shape[1] > width:
        out_ref[:, width:] = jnp.zeros((out_ref.shape[0], out_ref.shape[1] - width), out_ref.dtype)


def join(pieces, after=()):
    rows, width = pieces[0].shape
    padded = -(-width // LANES) * LANES
    return pl.pallas_call(
        functools.partial(join_kernel, count=len(pieces)),
        out_shape=jax.ShapeDtypeStruct((rows * len(pieces), padded), pieces[0].dtype),
        in_specs=[WHOLE] * len(pieces) + [pl.BlockSpec(memory_space=pl.ANY)] * len(after),
        out_specs=WHOLE,
        compiler_params=params(24),
        cost_estimate=cost(1),
        name="join",
    )(*pieces, *after)


def assemble_kernel(index_ref, mine_ref, other_ref, out_ref, *, relative, rows, shard_rows, step):
    wa, section = index_ref[0], index_ref[1]
    count = out_ref.shape[0] // shard_rows
    part = mine_ref.shape[0] // count
    width = out_ref.shape[1]
    for k in range(count):
        base = ((wa ^ k) if relative else k) * shard_rows
        start = pl.multiple_of(base + section * step, 16)
        out_ref[pl.ds(start, rows), :] = mine_ref[k * part : k * part + rows, :width]
        start = pl.multiple_of(base + (1 - section) * step, 16)
        out_ref[pl.ds(start, rows), :] = other_ref[k * part : k * part + rows, :width]


def assemble(index, mine, other, width, count, relative, rows, shard_rows, step):
    total = shard_rows * count
    return pl.pallas_call(
        functools.partial(
            assemble_kernel, relative=relative, rows=rows, shard_rows=shard_rows, step=step
        ),
        out_shape=jax.ShapeDtypeStruct((total, width), BF16),
        in_specs=[SCALARS, WHOLE, WHOLE],
        out_specs=WHOLE,
        compiler_params=params(24),
        cost_estimate=cost(2),
        name="assemble",
    )(index, mine, other)


def pair_kernel(index_ref, mine_ref, other_ref, out_ref, *, shard_rows):
    wa, section = index_ref[0], index_ref[1]
    width = mine_ref.shape[1]
    left = pl.multiple_of(section * width, LANES)
    right = pl.multiple_of((1 - section) * width, LANES)
    for k in range(out_ref.shape[0] // shard_rows):
        rows = pl.ds(pl.multiple_of((wa ^ k) * shard_rows, 16), shard_rows)
        piece = slice(k * shard_rows, (k + 1) * shard_rows)
        out_ref[rows, pl.ds(left, width)] = mine_ref[piece, :]
        out_ref[rows, pl.ds(right, width)] = other_ref[piece, :]


def assemble_pair(index, mine, other, shard_rows):
    total, width = mine.shape
    return pl.pallas_call(
        functools.partial(pair_kernel, shard_rows=shard_rows),
        out_shape=jax.ShapeDtypeStruct((total, 2 * width), BF16),
        in_specs=[SCALARS, WHOLE, WHOLE],
        out_specs=WHOLE,
        compiler_params=params(24),
        cost_estimate=cost(2.4),
        name="assemble_pair",
    )(index, mine, other)


def project_kernel(*refs, count):
    terms, refs = refs[:count], refs[count:]
    gain_ref, w_ref, cos_ref, sin_ref, u_ref, normed_ref, q_ref, kv_ref, mixed_ref = refs
    u = terms[0][...].astype(F32)
    for term in terms[1:]:
        u = u + term[...].astype(F32)
    u_ref[...] = u.astype(BF16)
    u = u_ref[...].astype(F32)
    scale = lax.rsqrt(jnp.mean(u * u, axis=-1, keepdims=True) + EPSILON)
    normed = (u * scale * gain_ref[...].astype(F32)).astype(BF16)
    normed_ref[...] = normed
    mixed_ref[:, : w_ref.shape[1]] = dot_nn(normed, w_ref[...])
    cosine, sine = cos_ref[...], sin_ref[...]
    lane = lane_of(cosine.shape)
    low = lane < HD
    roped = {}

    def unit(h, high):
        j = h // 2
        if j not in roped:
            block = mixed_ref[:, j * LANES : (j + 1) * LANES]
            if h < H + KVH:
                block = block * cosine + swap_halves(block, lane) * sine
            roped[j] = block
        return roped[j] if (h % 2 == 1) == high else pltpu.roll(roped[j], HD, 1)

    for h in range(H):
        padded = jnp.where(low, unit(h, False) * SCALE, 0.0)
        q_ref[:, h * LANES : (h + 1) * LANES] = padded.astype(BF16)
    for g in range(KVH):
        both = jnp.where(low, unit(H + g, False), unit(H + KVH + g, True))
        kv_ref[:, g * LANES : (g + 1) * LANES] = both.astype(BF16)


def project(terms, gain, weight, cosine, sine):
    rows, width = terms[0].shape
    count = len(terms)
    columns = weight.shape[1]
    padded = -(-columns // LANES) * LANES
    return pl.pallas_call(
        functools.partial(project_kernel, count=count),
        out_shape=(
            jax.ShapeDtypeStruct((rows, width), BF16),
            jax.ShapeDtypeStruct((rows, width), BF16),
            jax.ShapeDtypeStruct((rows, H * LANES), BF16),
            jax.ShapeDtypeStruct((rows, KVH * LANES), BF16),
        ),
        in_specs=[WHOLE] * (count + 4),
        out_specs=(WHOLE,) * 4,
        scratch_shapes=[pltpu.VMEM((rows, padded), F32)],
        compiler_params=params(24),
        cost_estimate=cost(2),
        name="project",
    )(*terms, gain, weight, cosine, sine)


def stack_heads(ref):
    return jnp.concatenate(
        [ref[:, i * LANES : (i + 1) * LANES] for i in range(GROUP)], axis=0
    )


def attend_kernel(qpos_ref, kpos_ref, q_ref, *refs):
    kv_refs, out_ref = refs[:-1], refs[-1]
    queries = stack_heads(q_ref)
    qpos = jnp.concatenate([qpos_ref[...]] * GROUP, axis=0)
    rows = queries.shape[0]
    top = jnp.full((rows, 1), MASKED, F32)
    total = jnp.zeros((rows, 1), F32)
    acc = jnp.zeros((rows, LANES), F32)
    for k, kv_ref in enumerate(kv_refs):
        for start in range(0, kv_ref.shape[0], KEY_CHUNK):
            size = min(KEY_CHUNK, kv_ref.shape[0] - start)
            kv = kv_ref[start : start + size, :]
            kpos = kpos_ref[k : k + 1, start : start + size]
            scores = jnp.where(kpos <= qpos, dot_nt(queries, kv), MASKED)
            new_top = jnp.maximum(top, jnp.max(scores, axis=-1, keepdims=True))
            fresh = jnp.exp(scores - new_top)
            decay = jnp.exp(top - new_top)
            total = total * decay + jnp.sum(fresh, axis=-1, keepdims=True)
            acc = acc * decay + dot_nn(fresh.astype(BF16), kv)
            top = new_top
    lse = top + jnp.log(total)
    out_ref[...] = jnp.where(lane_of(acc.shape) < HD, lse, acc / total)


def attend(qpos, kpos, queries, groups):
    rows = queries.shape[0]
    keys = groups[0].shape[0]
    pairs = H * rows * keys * len(groups)
    return pl.pallas_call(
        attend_kernel,
        out_shape=jax.ShapeDtypeStruct((H * rows, LANES), F32),
        grid=(KVH,),
        in_specs=[
            pl.BlockSpec((rows, 1), lambda g: (0, 0)),
            pl.BlockSpec(kpos.shape, lambda g: (0, 0)),
            pl.BlockSpec((rows, GROUP * LANES), lambda g: (0, g)),
        ]
        + [pl.BlockSpec((keys, LANES), lambda g: (0, g)) for _ in groups],
        out_specs=pl.BlockSpec((GROUP * rows, LANES), lambda g: (g, 0)),
        compiler_params=params(40),
        cost_estimate=cost(9.6),
        name="attend",
    )(qpos, kpos, queries, *groups)


def attend_back_kernel(qpos_ref, kpos_ref, q_ref, g_ref, o_ref, *refs, count):
    kv_refs, dq_ref, dkv_refs = refs[:count], refs[-count - 1], refs[-count:]
    queries = stack_heads(q_ref)
    grads = stack_heads(g_ref)
    saved = o_ref[...]
    lse = jnp.transpose(saved)[0:1, :]
    delta = jnp.sum(jnp.transpose(grads.astype(F32) * saved), axis=0, keepdims=True)
    qpos = jnp.concatenate([qpos_ref[...]] * GROUP, axis=1)
    rows = queries.shape[0]
    acc = jnp.zeros((rows, LANES), F32)
    for k, kv_ref in enumerate(kv_refs):
        for start in range(0, kv_ref.shape[0], KEY_CHUNK):
            size = min(KEY_CHUNK, kv_ref.shape[0] - start)
            kv = kv_ref[start : start + size, :]
            kpos = kpos_ref[start : start + size, k : k + 1]
            scores = jnp.where(kpos <= qpos, dot_nt(kv, queries), MASKED)
            probs = jnp.exp(scores - lse)
            grad_probs = dot_nt(kv, grads)
            grad_scores = (probs * (grad_probs - delta)).astype(BF16)
            acc = acc + dot_tn(grad_scores, kv)
            dkv = dot_nn(grad_scores, queries) + dot_nn(probs.astype(BF16), grads)
            dkv_refs[k][start : start + size, :] = dkv.astype(BF16)
    tok = q_ref.shape[0]
    for i in range(GROUP):
        dq_ref[:, i * LANES : (i + 1) * LANES] = acc[i * tok : (i + 1) * tok] * SCALE


def attend_back(qpos_row, kpos_column, queries, grads, saved, groups, after):
    rows = queries.shape[0]
    keys = groups[0].shape[0]
    pairs = H * rows * keys * len(groups)
    heads = pl.BlockSpec((rows, GROUP * LANES), lambda g: (0, g))
    kv_block = pl.BlockSpec((keys, LANES), lambda g: (0, g))
    result = pl.pallas_call(
        functools.partial(attend_back_kernel, count=len(groups)),
        out_shape=(jax.ShapeDtypeStruct((rows, H * LANES), F32),)
        + tuple(jax.ShapeDtypeStruct(group.shape, BF16) for group in groups),
        grid=(KVH,),
        in_specs=[
            pl.BlockSpec((1, rows), lambda g: (0, 0)),
            pl.BlockSpec(kpos_column.shape, lambda g: (0, 0)),
            heads,
            heads,
            pl.BlockSpec((GROUP * rows, LANES), lambda g: (g, 0)),
        ]
        + [kv_block for _ in groups]
        + [pl.BlockSpec(memory_space=pl.ANY) for _ in after],
        out_specs=(heads,) + tuple(kv_block for _ in groups),
        compiler_params=params(40),
        cost_estimate=cost(15.2),
        name="attend_back",
    )(qpos_row, kpos_column, queries, grads, saved, *groups, *after)
    return result[0], result[1:]


def close_kernel(u_ref, saved_ref, w_ref, gain_ref, low_ref, middle_ref, second_ref):
    rows = u_ref.shape[0]
    lane = lane_of((rows, LANES))
    for j in range(H // 2):
        even = pltpu.roll(saved_ref[2 * j * rows : (2 * j + 1) * rows, :], HD, 1)
        odd = saved_ref[(2 * j + 1) * rows : (2 * j + 2) * rows, :]
        low_ref[:, j * LANES : (j + 1) * LANES] = jnp.where(lane < HD, even, odd).astype(BF16)
    last = pltpu.roll(saved_ref[(H - 1) * rows : H * rows, :], HD, 1)
    low_ref[:, (H - 1) * HD : H * HD] = last[:, :HD].astype(BF16)
    middle = u_ref[...].astype(F32) + dot_nn(low_ref[...], w_ref[...])
    middle_ref[...] = middle
    scale = lax.rsqrt(jnp.mean(middle * middle, axis=-1, keepdims=True) + EPSILON)
    second_ref[...] = (middle * scale * gain_ref[...].astype(F32)).astype(BF16)


def close_attention(u, saved, weight, gain):
    rows, width = u.shape
    return pl.pallas_call(
        close_kernel,
        out_shape=(
            jax.ShapeDtypeStruct((rows, QW), BF16),
            jax.ShapeDtypeStruct((rows, width), F32),
            jax.ShapeDtypeStruct((rows, width), BF16),
        ),
        in_specs=[WHOLE] * 4,
        out_specs=(WHOLE,) * 3,
        compiler_params=params(24),
        cost_estimate=cost(1.4),
        name="close_attention",
    )(u, saved, weight, gain)


def widen_kernel(*refs, count):
    pieces, w_ref, wide_ref, hidden_ref = refs[:count], *refs[count:]
    second = jnp.concatenate([piece[...] for piece in pieces], axis=0)
    wide = dot_nn(second, w_ref[...])
    wide_ref[...] = wide
    half = wide.shape[1] // 2
    gate, up = wide[:, :half], wide[:, half:]
    hidden_ref[...] = (gate * jax.nn.sigmoid(gate) * up).astype(BF16)


def widen(pieces, weight):
    count = len(pieces)
    rows, width = pieces[0].shape
    columns = weight.shape[1]
    return pl.pallas_call(
        functools.partial(widen_kernel, count=count),
        out_shape=(
            jax.ShapeDtypeStruct((count * rows, columns), F32),
            jax.ShapeDtypeStruct((count * rows, columns // 2), BF16),
        ),
        in_specs=[WHOLE] * (count + 1),
        out_specs=(WHOLE,) * 2,
        compiler_params=params(40),
        cost_estimate=cost(2.5),
        name="widen",
    )(*pieces, weight)


def narrow_kernel(hidden_ref, down_ref, later_ref, *outs):
    rows = outs[0].shape[0]
    for k, out in enumerate(outs):
        part = hidden_ref[k * rows : (k + 1) * rows, :]
        out[...] = dot_nt(part, down_ref[...]).astype(out.dtype)


def narrow(hidden, down, count, later):
    rows, width = hidden.shape[0] // count, down.shape[0]
    return pl.pallas_call(
        narrow_kernel,
        out_shape=(jax.ShapeDtypeStruct((rows, width), F32),)
        + tuple(jax.ShapeDtypeStruct((rows, width), BF16) for _ in range(count - 1)),
        in_specs=[WHOLE, WHOLE, pl.BlockSpec(memory_space=pl.ANY)],
        out_specs=(WHOLE,) * count,
        compiler_params=params(24),
        cost_estimate=cost(1.7),
        name="narrow",
    )(hidden, down, later)


def mlp_back_kernel(*refs, count):
    pieces, wide_ref, w_ref, down_ref = refs[:count], *refs[count : count + 3]
    grads_ref, outs = refs[count + 3], refs[count + 4 :]
    rows = pieces[0].shape[0]
    grad_y = jnp.concatenate([piece[...] for piece in pieces], axis=0)
    grad_hidden = dot_nn(grad_y, down_ref[...])
    half = wide_ref.shape[1] // 2
    gate, up = wide_ref[:, :half], wide_ref[:, half:]
    sig = jax.nn.sigmoid(gate)
    grads_ref[:, :half] = (grad_hidden * up * sig * (1.0 + gate * (1.0 - sig))).astype(BF16)
    grads_ref[:, half:] = (grad_hidden * gate * sig).astype(BF16)
    partial = dot_nt(grads_ref[...], w_ref[...])
    for k, out in enumerate(outs):
        out[...] = partial[k * rows : (k + 1) * rows].astype(out.dtype)


def mlp_back(pieces, wide, weight, down):
    count = len(pieces)
    rows, width = pieces[0].shape
    columns = weight.shape[1]
    result = pl.pallas_call(
        functools.partial(mlp_back_kernel, count=count),
        out_shape=(
            jax.ShapeDtypeStruct((count * rows, columns), BF16),
            jax.ShapeDtypeStruct((rows, width), F32),
        )
        + tuple(jax.ShapeDtypeStruct((rows, width), BF16) for _ in range(count - 1)),
        in_specs=[WHOLE] * (count + 3),
        out_specs=(WHOLE,) * (count + 1),
        compiler_params=params(40),
        cost_estimate=cost(4),
        name="mlp_back",
    )(*pieces, wide, weight, down)
    return result[0], result[1:]


def norm_back(values, gain, gradient):
    scaling = lax.rsqrt(jnp.mean(values * values, axis=-1, keepdims=True) + EPSILON)
    gain_grad = jnp.sum(gradient * values * scaling, axis=0, keepdims=True)
    scaled = gradient * gain.astype(F32)
    inner = jnp.mean(scaled * values, axis=-1, keepdims=True)
    return gain_grad, scaling * scaled - values * (scaling * scaling * scaling) * inner


def open_back_kernel(*refs, count):
    terms = refs[:count]
    middle_ref, gain_ref, y_ref, w_ref = refs[count : count + 4]
    grad_ref, low_ref, padded_ref, gain_grad_ref, wide_ref = refs[count + 4 :]
    gradient = terms[0][...]
    for term in terms[1:]:
        gradient = gradient + term[...].astype(F32)
    gain_grad, through = norm_back(middle_ref[...], gain_ref[...], gradient)
    gain_grad_ref[...] = gain_grad
    grad_middle = y_ref[...].astype(F32) + through
    grad_ref[...] = grad_middle
    low = grad_middle.astype(BF16)
    low_ref[...] = low
    wide_ref[:, :QW] = dot_nt(low, w_ref[...])
    lane = lane_of((low.shape[0], LANES))
    for h in range(H):
        block = wide_ref[:, h // 2 * LANES : (h // 2 + 1) * LANES]
        placed = block if h % 2 else pltpu.roll(block, HD, 1)
        padded_ref[:, h * LANES : (h + 1) * LANES] = jnp.where(lane < HD, 0.0, placed).astype(BF16)


def open_back(terms, middle, gain, grad_y, weight):
    rows, width = middle.shape
    count = len(terms)
    return pl.pallas_call(
        functools.partial(open_back_kernel, count=count),
        out_shape=(
            jax.ShapeDtypeStruct((rows, width), F32),
            jax.ShapeDtypeStruct((rows, width), BF16),
            jax.ShapeDtypeStruct((rows, H * LANES), BF16),
            jax.ShapeDtypeStruct((1, width), F32),
        ),
        in_specs=[WHOLE] * (count + 4),
        out_specs=(WHOLE,) * 4,
        scratch_shapes=[pltpu.VMEM((rows, (H + 1) // 2 * LANES), F32)],
        compiler_params=params(24),
        cost_estimate=cost(2),
        name="open_back",
    )(*terms, middle, gain, grad_y, weight)


def turned_back(block, cosine, sine, lane):
    return block * cosine - swap_halves(block, lane) * sine


def query_back_kernel(dq_ref, cos_ref, sin_ref, w_ref, mixed_ref, part_ref):
    cosine, sine = cos_ref[...], sin_ref[...]
    lane = lane_of(cosine.shape)

    def head(h):
        return turned_back(dq_ref[:, h * LANES : (h + 1) * LANES], cosine, sine, lane)

    for j in range(H // 2):
        block = jnp.where(lane < HD, head(2 * j), pltpu.roll(head(2 * j + 1), HD, 1))
        mixed_ref[:, j * LANES : (j + 1) * LANES] = block.astype(BF16)
    mixed_ref[:, (H - 1) * HD : QW] = head(H - 1)[:, :HD].astype(BF16)
    part_ref[...] = dot_nt(mixed_ref[...], w_ref[:, :QW])


def query_back(dq, cosine, sine, weight):
    rows, width = dq.shape[0], weight.shape[0]
    return pl.pallas_call(
        query_back_kernel,
        out_shape=(
            jax.ShapeDtypeStruct((rows, QW), BF16),
            jax.ShapeDtypeStruct((rows, width), F32),
        ),
        in_specs=[WHOLE] * 4,
        out_specs=(WHOLE,) * 2,
        compiler_params=params(24),
        cost_estimate=cost(1.2),
        name="query_back",
    )(dq, cosine, sine, weight)


def key_back_kernel(*refs, count):
    terms = refs[:count]
    part_ref, cos_ref, sin_ref, w_ref, u_ref, gain_ref, middle_ref = refs[count : count + 7]
    mixed_ref, out_ref, gain_grad_ref, wide_ref = refs[count + 7 :]
    grad_kv = terms[0][...].astype(F32)
    for term in terms[1:]:
        grad_kv = grad_kv + term[...].astype(F32)
    cosine, sine = cos_ref[...], sin_ref[...]
    lane = lane_of(cosine.shape)
    low = lane < HD
    blocks = [grad_kv[:, g * LANES : (g + 1) * LANES] for g in range(KVH)]
    keys = [turned_back(block, cosine, sine, lane) for block in blocks]

    def unit(h, high):
        block, at_high = (keys[h], False) if h < KVH else (blocks[h - KVH], True)
        return block if at_high == high else pltpu.roll(block, HD, 1)

    for j in range(KVH):
        block = jnp.where(low, unit(2 * j, False), unit(2 * j + 1, True))
        mixed_ref[:, j * LANES : (j + 1) * LANES] = block.astype(BF16)
    for j in range(KVH + 1):
        left = unit(2 * j - 1, False) if j else jnp.zeros(cosine.shape, F32)
        block = jnp.where(low, left, unit(2 * j, True)) if j < KVH else left
        wide_ref[:, j * LANES : (j + 1) * LANES] = block.astype(BF16)
    begin = QW // LANES * LANES
    columns = w_ref.shape[1] - begin
    gradient = part_ref[...] + dot_nt(wide_ref[:, :columns], w_ref[:, begin:])
    gain_grad, through = norm_back(u_ref[...].astype(F32), gain_ref[...], gradient)
    gain_grad_ref[...] = gain_grad
    out_ref[...] = (middle_ref[...] + through).astype(BF16)


def key_back(terms, part, cosine, sine, weight, u, gain, grad_middle):
    rows, width = u.shape
    count = len(terms)
    return pl.pallas_call(
        functools.partial(key_back_kernel, count=count),
        out_shape=(
            jax.ShapeDtypeStruct((rows, 2 * KW), BF16),
            jax.ShapeDtypeStruct((rows, width), BF16),
            jax.ShapeDtypeStruct((1, width), F32),
        ),
        in_specs=[WHOLE] * (count + 7),
        out_specs=(WHOLE,) * 3,
        scratch_shapes=[pltpu.VMEM((rows, 2 * KW + LANES), BF16)],
        compiler_params=params(24),
        cost_estimate=cost(2),
        name="key_back",
    )(*terms, part, cosine, sine, weight, u, gain, grad_middle)


def finish_kernel(index_ref, mine_ref, other_ref, gate_ref, up_ref):
    wa, first = index_ref[0], index_ref[1] == 0
    rows = gate_ref.shape[0]
    width = mine_ref.shape[1]
    for k in range(mine_ref.shape[0] // rows):
        columns = pl.ds(pl.multiple_of((wa ^ k) * width, LANES), width)
        piece = slice(k * rows, (k + 1) * rows)
        mine, other = mine_ref[piece, :].astype(F32), other_ref[piece, :].astype(F32)
        gate_ref[:, columns] = jnp.where(first, mine, other)
        up_ref[:, columns] = jnp.where(first, other, mine)


def finish(index, mine, other, rows):
    total, width = mine.shape
    result = jax.ShapeDtypeStruct((rows, total // rows * width), F32)
    return pl.pallas_call(
        finish_kernel,
        out_shape=(result, result),
        in_specs=[SCALARS, WHOLE, WHOLE],
        out_specs=(WHOLE, WHOLE),
        compiler_params=params(24),
        cost_estimate=cost(3.3),
        name="finish",
    )(index, mine, other)


def to_sibling(value):
    return lax.ppermute(value, "section", [(0, 1), (1, 0)])


def to_peer(value, k):
    count = lax.axis_size("wa")
    return lax.ppermute(value, "wa", [(i, i ^ k) for i in range(count)])


def gather_wa(value):
    return [value] + [to_peer(value, k) for k in range(1, lax.axis_size("wa"))]


def send_wa(pieces):
    return [pieces[0]] + [to_peer(piece, k) for k, piece in enumerate(pieces) if k]


def rotates(count):
    return count <= 4


def gather_ctx(value):
    count = lax.axis_size("ctx")
    if not rotates(count):
        return lax.all_gather(value, "ctx", axis=0, tiled=True)
    pieces = [value]
    for k in range(1, count):
        pieces.append(lax.ppermute(value, "ctx", [(i, (i + k) % count) for i in range(count)]))
    return join(pieces)


def scatter_ctx(value):
    count = lax.axis_size("ctx")
    rows = value.shape[0] // count
    if not rotates(count):
        blocks = value.reshape(count, rows, value.shape[1])
        return list(lax.all_to_all(blocks, "ctx", 0, 0, tiled=True))
    pieces = [value[:rows]]
    for k in range(1, count):
        piece = value[k * rows : (k + 1) * rows]
        pieces.append(lax.ppermute(piece, "ctx", [(i, (i - k) % count) for i in range(count)]))
    return pieces


def at(value, index, size, dim):
    return lax.dynamic_slice_in_dim(value, index * size, size, dim)


def tie(values, after):
    values, after = tuple(values), tuple(after)
    anywhere = pl.BlockSpec(memory_space=pl.ANY)
    return pl.pallas_call(
        lambda *refs: None,
        out_shape=tuple(jax.ShapeDtypeStruct(value.shape, value.dtype) for value in values),
        in_specs=[anywhere] * (len(values) + len(after)),
        out_specs=(anywhere,) * len(values),
        input_output_aliases={i: i for i in range(len(values))},
        cost_estimate=cost(0),
        name="tie",
    )(*values, *after)


def added(terms):
    total = terms[0].astype(F32)
    for term in terms[1:]:
        total = total + term.astype(F32)
    return total


def per_device(
    block_input, out_cotangent, block_table, attn_gain, w_qkv, w_out, mlp_gain, w_gate, w_up, w_down
):
    section = lax.axis_index("section")
    wa = lax.axis_index("wa")
    ctx = lax.axis_index("ctx")
    wa_count = lax.axis_size("wa")
    ctx_count = lax.axis_size("ctx")
    layers = lax.axis_size("section")
    first = section == 0
    peers = range(wa_count)
    index = jnp.stack([wa, section]).astype(jnp.int32)
    micro_count, tok_rows, width = block_input.shape
    half_rows = tok_rows // 2
    shard_rows = w_qkv.shape[1]
    ff_part = w_down.shape[1]
    w_qkv, w_out, w_gate, w_up, w_down = (a[0] for a in (w_qkv, w_out, w_gate, w_up, w_down))
    w_down = w_down.T

    in_block = jnp.arange(half_rows, dtype=jnp.int32)
    table = block_table.reshape(-1, 2)

    def positions_of(devices):
        return (table[devices][..., None] * half_rows + in_block).reshape(-1)

    own_pos = positions_of((ctx * wa_count + wa)[None])
    steps = jnp.arange(ctx_count)
    sources = (ctx - steps) % ctx_count if rotates(ctx_count) else steps
    key_pos = jnp.stack([positions_of(sources * wa_count + (wa ^ k)) for k in peers])
    key_pos_column = key_pos.T
    qpos_column, qpos_row = own_pos[:, None], own_pos[None, :]
    inverse = ROPE_BASE ** (-(jnp.arange(HD // 2, dtype=F32) * 2.0) / HD)
    angles = own_pos.astype(F32)[:, None] * inverse[None, :]
    cosine = jnp.tile(jnp.cos(angles), (1, 2 * LANES // HD))
    sines = jnp.sin(angles)
    sine = jnp.tile(jnp.concatenate([-sines, sines], axis=1), (1, LANES // HD))

    kept_rows = shard_rows // 2 + 8
    step = shard_rows - kept_rows
    own_gains = jnp.concatenate([attn_gain, mlp_gain], axis=0)
    gain_rows = jnp.pad(own_gains, ((0, 14), (0, w_qkv.shape[1] - shard_rows)))

    def halves(shard, extra=None):
        def part(half):
            rows = lax.dynamic_slice_in_dim(shard, half * step, kept_rows, 0)
            return rows if extra is None else jnp.concatenate([rows, extra], axis=0)

        keep, other = part(section), to_sibling(part(1 - section))
        return jnp.where(first, keep, other), jnp.where(first, other, keep)

    def fetch_rows(part, after=()):
        if after:
            (part,) = tie((part,), after)
        return gather_wa(part)

    def placed_rows(pieces, after=()):
        mine = join(pieces, after)
        columns = pieces[0].shape[1]
        return assemble(
            index, mine, to_sibling(mine), columns, wa_count, True, kept_rows, shard_rows, step
        )

    def gains_of(pieces):
        rows = jnp.stack([piece[kept_rows : kept_rows + 2, :shard_rows] for piece in pieces])
        return rows[wa ^ jnp.arange(wa_count)].transpose(1, 0, 2).reshape(2, 1, width)

    def fetch_columns(part, after):
        return send_wa(tie([at(part, wa ^ k, ff_part, 1) for k in peers], after))

    def placed_columns(pieces, after):
        mine = join(pieces, after)
        return assemble_pair(index, mine, to_sibling(mine), shard_rows)

    qkv_parts = halves(w_qkv, gain_rows)
    qkv_pieces = fetch_rows(qkv_parts[0])
    qkv = placed_rows(qkv_pieces)
    out_parts = halves(w_out)
    crossing = to_sibling(jnp.where(first, w_up, w_gate))
    wide_parts = (jnp.where(first, w_gate, crossing), jnp.where(first, crossing, w_up))
    down_other = to_sibling(w_down)
    downs = (jnp.where(first, w_down, down_other), jnp.where(first, down_other, w_down))
    out_pieces = fetch_rows(out_parts[0], qkv_pieces[1:])
    last_pieces = fetch_rows(qkv_parts[1], out_pieces[1:])
    gains = [gains_of(qkv_pieces), gains_of(last_pieces)]
    qkvs, outs, wides = [qkv], [], []

    terms = [lax.dynamic_index_in_dim(block_input, section, 0, keepdims=False)]
    cotangent = lax.dynamic_index_in_dim(out_cotangent, section, 0, keepdims=False)
    records, inputs = [], []
    for layer in range(layers):
        u, normed, queries, kv = project(terms, gains[layer][0], qkvs[layer], cosine, sine)
        pieces = last_pieces[1:]
        if layer:
            out_pieces = fetch_rows(out_parts[layer], terms[1:])
            (grad_y,) = tie((cotangent,), out_pieces[1:])
            grad_ys = gather_wa(grad_y)
            pieces = grad_ys[1:]
        group = gather_ctx(kv)
        outs.append(placed_rows(out_pieces, (group,)))
        (group,) = tie((group,), pieces)
        groups = gather_wa(group)
        wide_pieces = fetch_columns(wide_parts[layer], groups[1:])
        saved = attend(qpos_column, key_pos, queries, groups)
        wides.append(placed_columns(wide_pieces, (saved,)))
        if not layer:
            qkvs.append(placed_rows(last_pieces, (saved,)))
        low, middle, second = close_attention(u, saved, outs[layer], gains[layer][1])
        seconds = gather_wa(*tie((second,), wide_pieces[1:]))
        wide, hidden = widen(seconds, wides[layer])
        if layer < layers - 1:
            partial = narrow(hidden, downs[layer], wa_count, index)
            terms = [middle] + send_wa(partial)
        inputs.append(u)
        records.append((u, normed, queries, groups, saved, low, middle, seconds, wide, hidden))

    def over_cores(value, size, dim):
        keep = at(value, section, size, dim)
        other = to_sibling(at(value, 1 - section, size, dim))
        return (keep.astype(F32) + other.astype(F32)).astype(BF16)

    def blocked(value):
        return value.reshape(wa_count, 2, shard_rows // 2, value.shape[1])

    def rows_over_wa(blocks, after):
        half = over_cores(blocks, 1, 1)[:, 0]
        pieces = [at(half, wa ^ k, 1, 0)[0] for k in peers]
        pieces = send_wa(tie(pieces, after) if after else pieces)
        return added(pieces).astype(BF16), pieces[1:]

    def over_ctx(values, turn):
        order = [(i + turn) % ctx_count for i in range(ctx_count)]
        return lax.psum(tuple(values), "ctx", axis_index_groups=[order])

    input_grads, gain_grads = [None] * layers, []
    sums, pending = {}, ()
    for layer in reversed(range(layers)):
        u, normed, queries, groups, saved, low, middle, seconds, wide, hidden = records[layer]
        if layer < layers - 1:
            grad_ys = gather_wa(grad_y)
        grad_wide, partial = mlp_back(grad_ys, wide, wides[layer], downs[layer])
        terms = send_wa(partial)
        grad_middle, grad_low, grad_heads, gain_two_grad = open_back(
            terms, middle, gains[layer][1], grad_y, outs[layer]
        )

        wide_grad = dot_tn(jnp.concatenate(seconds, axis=0), grad_wide).astype(BF16)
        down_grad = dot_tn(jnp.concatenate(grad_ys, axis=0), hidden).astype(BF16)
        wide_half = over_cores(wide_grad, ff_part, 1)
        down_half = over_cores(down_grad, width // 2, 0)
        pieces = [at(wide_half, wa ^ k, shard_rows, 0) for k in peers]
        pieces = send_wa(pieces)
        wide_rows = join(pieces)
        wide_pieces = pieces[1:]
        before = (wide_rows, down_half)
        if pending:
            key_half, _ = rows_over_wa(pending[0], ())
            before = (wide_rows, key_half)

        dq, dkv = attend_back(
            qpos_row, key_pos_column, queries, grad_heads, saved, groups, before
        )
        if layer < layers - 1:
            dkv = tie(dkv, done)
        dkv = send_wa(dkv)
        gathered = added(dkv).astype(BF16)
        if layer == layers - 1:
            done = over_ctx((wide_rows, down_half), 0)
            sums["wide", layer], sums["down", layer] = done
        else:
            done = over_ctx((key_half, wide_rows, down_half), 1)
            sums["key", layer + 1], sums["wide", layer], sums["down", layer] = done
            last_square = square_half

        terms = scatter_ctx(gathered)
        grad_query, part = query_back(dq, cosine, sine, qkvs[layer])
        out_grad = dot_tn(low, grad_low).astype(BF16)
        query_grad = dot_tn(normed, grad_query).astype(BF16)
        square_grad = jnp.concatenate([blocked(out_grad), blocked(query_grad)], axis=2)
        square_half, square_pieces = rows_over_wa(square_grad, ())
        if layer == 0:
            done = over_ctx((last_square, square_half), 2)
            sums["square", layer + 1], sums["square", layer] = done

        grad_key, grad_u, gain_one_grad = key_back(
            terms, part, cosine, sine, qkvs[layer], u, gains[layer][0], grad_middle
        )
        key_grad = blocked(dot_tn(normed, grad_key).astype(BF16))
        pending = (key_grad,)
        gain_grads = [gain_one_grad, gain_two_grad] + gain_grads
        input_grads[layer] = grad_u
        grad_y = grad_u

    tails = jnp.concatenate(gain_grads, axis=0).reshape(-1, wa_count, 1, shard_rows)
    tails = jnp.broadcast_to(
        tails.transpose(1, 2, 0, 3).astype(BF16), (wa_count, 2, 2 * layers, shard_rows)
    )
    tails = jnp.pad(tails, ((0, 0), (0, 0), (0, 4), (0, 2 * KW - shard_rows)))
    packed, pieces = rows_over_wa(jnp.concatenate([key_grad, tails], axis=2), square_pieces)
    if rotates(ctx_count):
        key_half = added(jnp.split(gather_ctx(packed), ctx_count, axis=0))
    else:
        key_half = lax.psum(packed, "ctx").astype(F32)
    gain_sums = key_half[shard_rows // 2 : shard_rows // 2 + 2 * layers, :shard_rows]
    sums["key", 0] = key_half[: shard_rows // 2].astype(BF16)

    hidden, middle = records[-1][-1], records[-1][6]
    partial = narrow(hidden, downs[-1], wa_count, pieces[-1])
    last_result = added([middle] + send_wa(partial)).astype(BF16)

    def swapped(values):
        mine = jnp.where(first, values[0], values[1])
        return mine, to_sibling(jnp.where(first, values[1], values[0]))

    def by_layer(values):
        mine, other = swapped(values)
        return jnp.where(first, mine, other), jnp.where(first, other, mine)

    def both(values):
        return jnp.stack(by_layer(values))[None]

    def halves_of(name):
        return [sums[name, layer] for layer in range(layers)]

    down_halves, square_halves, key_halves = (
        by_layer(halves_of(name)) for name in ("down", "square", "key")
    )
    gate_sum, up_sum = finish(index, *swapped(halves_of("wide")), shard_rows)
    half = shard_rows // 2
    out_sum = jnp.concatenate([part[:half] for part in square_halves], axis=0)
    query_sum = jnp.concatenate([part[half:] for part in square_halves], axis=0)
    qkv_sum = jnp.concatenate([query_sum, jnp.concatenate(key_halves, axis=0)], axis=1)
    gain_own = lax.dynamic_index_in_dim(gain_sums.reshape(layers, 2, shard_rows), section, 0)
    return (
        both([inputs[1], last_result]),
        both(input_grads),
        gain_own[:, 0],
        qkv_sum.astype(F32)[None],
        out_sum.astype(F32)[None],
        gain_own[:, 1],
        gate_sum[None],
        up_sum[None],
        jnp.concatenate(down_halves, axis=0).astype(F32).T[None],
    )


def solution(mesh):
    return jax.shard_map(
        per_device,
        mesh=mesh,
        in_specs=(
            P(None, ("ctx", "wa"), None),
            P(None, ("ctx", "wa"), None),
            P(),
            P("section", "wa"),
            P("section", "wa", None),
            P("section", "wa", None),
            P("section", "wa"),
            P("section", "wa", None),
            P("section", "wa", None),
            P("section", "wa", None),
        ),
        out_specs=(
            P("section", None, ("ctx", "wa"), None),
            P("section", None, ("ctx", "wa"), None),
            P("section", "wa"),
            P("section", "wa", None),
            P("section", "wa", None),
            P("section", "wa"),
            P("section", "wa", None),
            P("section", "wa", None),
            P("section", "wa", None),
        ),
        check_vma=False,
    )
```
